512 devices in a mesh: gy: 16 (over y, x), gz: 32 (over z, core).
Axes of the slice: x: 4, y: 4, z: 16, core: 2. Of those that a mesh axis runs over, the one named last changes fastest.
Arguments:
- conduct: float32 [256, 1024, 128], P('gy', 'gz'), may hold values from 0.3 to 3
- seeds: int32 [256, 1024, 128], P('gy', 'gz'), may hold values 0 or 1
- labels: int32 [256, 1024, 128], P('gy', 'gz'), may hold values 0 or 1
- start: float32 [256, 1024, 128], P('gy', 'gz'), may hold values from 0 to 1
- cotangent: float32 [256, 1024, 128], P('gy', 'gz'), may hold values from -12 to 12
Outputs:
- probability: float32 [256, 1024, 128], P('gy', 'gz')
- adjoint: float32 [256, 1024, 128], P('gy', 'gz')
- grad_conduct: float32 [256, 1024, 128], P('gy', 'gz')
The draws below stay inside these ranges and needn't reach their ends.
All inputs are finite; a program needn't handle non-finite values. No bound on the sum of `seeds` or of `labels` on one device may be relied on, other than what follows from the above.
Results may differ from the reference program's by a relative error of at most 0.0001.
Values sent between devices are 32-bit elements; how exact they have to be, the bound alone decides.
No kernel may reach another device: no remote copies, remote signals or barrier semaphores. Data moves between devices by JAX's collectives and lax.ppermute only.
A program may use at most 64 MiB of HBM per device.

```python
import math
import jax
import jax.numpy as jnp

NX = 128
ITERS = 2
NY = 256
NZ = 1024


def draw_cotangent(key, part):
    rows = jnp.arange(NY, dtype=jnp.float32) / max(NY - 1, 1)
    values = jnp.clip(jax.random.normal(key, (NY, NZ, NX), jnp.float32), -4.0, 4.0)
    return values * (1.0 + 2.0 * rows)[:, None, None]


def plant(array, key, least, top_value):
    longest = array.shape.index(max(array.shape))
    spots = []
    for shift in (0, 1):
        where = [jax.random.randint(jax.random.fold_in(key, axis), (), 0, length) for axis, length in enumerate(array.shape)]
        where[longest] = (where[longest] + shift) % array.shape[longest]
        spots.append(tuple(where))
    return array.at[spots[0]].set(least).at[spots[1]].set(top_value)


def level_of(rng, extent, cuts, least, top_value):
    factor_of = 1.0
    for dim, blocks in cuts:
        heights = jax.random.uniform(jax.random.fold_in(jax.random.fold_in(rng, 6), dim), (blocks,), jnp.float32, least / len(cuts), top_value / len(cuts))
        factor_of = factor_of * jnp.repeat(jnp.exp(heights), extent[dim] // blocks).reshape((-1,) + (1,) * (len(extent) - 1 - dim))
    return factor_of


def setup_inputs(seed: int = 0) -> dict:
    streams_of = jax.random.split(jax.random.key(seed), 6)
    return {
        "conduct": jnp.clip(jnp.exp(math.log(3.0) - 2.3025851 * jax.random.uniform(streams_of[0], (NY, NZ, NX), jnp.float32) ** level_of(streams_of[0], (NY, NZ, NX), ((0, 16), (1, 32)), -0.2, 0.2)), 0.3, 3.0),
        "seeds": plant((jax.random.randint(streams_of[1], (NY, NZ, NX), 0, 8) < 1).astype(jnp.int32), jax.random.fold_in(streams_of[1], 1), 0, 1),
        "labels": plant((jax.random.randint(streams_of[2], (NY, NZ, NX), 0, 2) < 1).astype(jnp.int32), jax.random.fold_in(streams_of[2], 1), 0, 1),
        "start": jnp.clip(1.0 * jax.random.uniform(streams_of[3], (NY, NZ, NX), jnp.float32) ** level_of(streams_of[3], (NY, NZ, NX), ((0, 16), (1, 32)), -0.2, 0.2), 0.0, 1.0),
        "cotangent": draw_cotangent(jax.random.fold_in(streams_of[5], 71), 0),
    }


seed_pull = 4.0
screening = 0.05


def harmonic(first, second):
    return 2.0 * first * second / (first + second)


def pad_sides(field):
    return jnp.pad(field, ((1, 1), (1, 1), (0, 0)))


def coefficients(padded_cond, seeds):
    core = padded_cond[1:-1, 1:-1]
    along = jnp.pad(core, ((0, 0), (0, 0), (1, 1)))
    weights = (harmonic(core, padded_cond[2:, 1:-1]), harmonic(core, padded_cond[:-2, 1:-1]),
               harmonic(core, padded_cond[1:-1, 2:]), harmonic(core, padded_cond[1:-1, :-2]),
               harmonic(core, along[..., 2:]), harmonic(core, along[..., :-2]))
    diagonal = weights[0] + weights[1] + weights[2] + weights[3] + weights[4] + weights[5]
    diagonal = diagonal + seed_pull * seeds.astype(jnp.float32) + screening
    return (diagonal,) + weights


def operate(padded, coeffs):
    field = padded[1:-1, 1:-1]
    along = jnp.pad(field, ((0, 0), (0, 0), (1, 1)))
    out = coeffs[0] * field - coeffs[1] * padded[2:, 1:-1] - coeffs[2] * padded[:-2, 1:-1]
    out = out - coeffs[3] * padded[1:-1, 2:] - coeffs[4] * padded[1:-1, :-2]
    return out - coeffs[5] * along[..., 2:] - coeffs[6] * along[..., :-2]


def edge_term(ci, cj, ui, uj, vi, vj):
    total = ci + cj
    return -2.0 * cj * cj / (total * total) * (ui - uj) * (vi - vj)


def gradient(cond_pad, prob_pad, adj_pad):
    ci = cond_pad[1:-1, 1:-1]
    ui = prob_pad[1:-1, 1:-1]
    vi = adj_pad[1:-1, 1:-1]
    out = edge_term(ci, cond_pad[2:, 1:-1], ui, prob_pad[2:, 1:-1], vi, adj_pad[2:, 1:-1])
    out = out + edge_term(ci, cond_pad[:-2, 1:-1], ui, prob_pad[:-2, 1:-1], vi, adj_pad[:-2, 1:-1])
    out = out + edge_term(ci, cond_pad[1:-1, 2:], ui, prob_pad[1:-1, 2:], vi, adj_pad[1:-1, 2:])
    out = out + edge_term(ci, cond_pad[1:-1, :-2], ui, prob_pad[1:-1, :-2], vi, adj_pad[1:-1, :-2])
    cx = jnp.pad(ci, ((0, 0), (0, 0), (1, 1)))
    ux = jnp.pad(ui, ((0, 0), (0, 0), (1, 1)))
    vx = jnp.pad(vi, ((0, 0), (0, 0), (1, 1)))
    out = out + edge_term(ci, cx[..., 2:], ui, ux[..., 2:], vi, vx[..., 2:])
    return out + edge_term(ci, cx[..., :-2], ui, ux[..., :-2], vi, vx[..., :-2])


def conjugate(iterate, resid, coeffs):
    direction = resid
    norm_now = jnp.sum(resid * resid)
    for step in range(ITERS):
        image = operate(pad_sides(direction), coeffs)
        alpha = norm_now / jnp.sum(direction * image)
        iterate = iterate + alpha * direction
        resid = resid - alpha * image
        norm_next = jnp.sum(resid * resid)
        direction = resid + (norm_next / norm_now) * direction
        norm_now = norm_next
    return iterate


def reference(conduct, seeds, labels, start, cotangent):
    cond_pad = pad_sides(conduct)
    coeffs = coefficients(cond_pad, seeds)
    rhs = seed_pull * (seeds * labels).astype(jnp.float32)
    probability = conjugate(start, rhs - operate(pad_sides(start), coeffs), coeffs)
    adjoint = conjugate(jnp.zeros_like(cotangent), cotangent, coeffs)
    grad_conduct = gradient(cond_pad, pad_sides(probability), pad_sides(adjoint))
    return probability, adjoint, grad_conduct
```

```python
import jax
import jax.numpy as jnp
from jax import lax
from jax.sharding import Mesh
from jax.sharding import PartitionSpec as P

GY = ("gy_0", "gy_1")
GZ = ("gz_0", "gz_1")

seed_pull = 4.0
screening = 0.05


def neighbours(last, first, axis):
    devices = lax.axis_size(axis)
    up = [(i, i + 1) for i in range(devices - 1)]
    return lax.ppermute(last, axis, up), lax.ppermute(first, axis, [(b, a) for a, b in up])


def extend(fields, widths, axis, dim):
    def face(f, w, end):
        n = f.shape[dim]
        part = lax.slice_in_dim(f, n - w if end else 0, n if end else w, axis=dim)
        other = 1 - dim
        short = fields[0].shape[other] - f.shape[other]
        return jnp.pad(part, [(short // 2, short // 2) if d == other else (0, 0) for d in range(3)])

    last = jnp.concatenate([face(f, w, True) for f, w in zip(fields, widths)], axis=dim)
    first = jnp.concatenate([face(f, w, False) for f, w in zip(fields, widths)], axis=dim)
    low, high = neighbours(last, first, axis)
    out, at = [], 0
    for f, w in zip(fields, widths):
        other = 1 - dim
        short = (fields[0].shape[other] - f.shape[other]) // 2
        a = lax.slice_in_dim(low, at, at + w, axis=dim)
        b = lax.slice_in_dim(high, at, at + w, axis=dim)
        a = lax.slice_in_dim(a, short, a.shape[other] - short, axis=other)
        b = lax.slice_in_dim(b, short, b.shape[other] - short, axis=other)
        out.append(jnp.concatenate([a, f, b], axis=dim))
        at += w
    return out


def over_copies(shard, axis):
    copies = jnp.broadcast_to(shard, (lax.axis_size(axis), *shard.shape))
    return jnp.sum(lax.all_to_all(copies, axis, split_axis=0, concat_axis=0, tiled=True), axis=0)


def harmonic(first, second):
    return 2.0 * first * second / jnp.maximum(first + second, 1e-30)


def coefficients(padded_cond, seeds):
    core = padded_cond[1:-1, 1:-1]
    along = jnp.pad(core, ((0, 0), (0, 0), (1, 1)))
    weights = (
        harmonic(core, padded_cond[2:, 1:-1]),
        harmonic(core, padded_cond[:-2, 1:-1]),
        harmonic(core, padded_cond[1:-1, 2:]),
        harmonic(core, padded_cond[1:-1, :-2]),
        harmonic(core, along[..., 2:]),
        harmonic(core, along[..., :-2]),
    )
    diagonal = weights[0] + weights[1] + weights[2] + weights[3] + weights[4] + weights[5]
    diagonal = diagonal + seed_pull * seeds + screening
    return (diagonal,) + weights


def inner(arrays, n):
    return tuple(a[n:-n, n:-n] for a in arrays)


def operate(padded, coeffs):
    field = padded[1:-1, 1:-1]
    along = jnp.pad(field, ((0, 0), (0, 0), (1, 1)))
    out = coeffs[0] * field - coeffs[1] * padded[2:, 1:-1] - coeffs[2] * padded[:-2, 1:-1]
    out = out - coeffs[3] * padded[1:-1, 2:] - coeffs[4] * padded[1:-1, :-2]
    return out - coeffs[5] * along[..., 2:] - coeffs[6] * along[..., :-2]


def edge_term(ci, cj, ui, uj, vi, vj):
    total = ci + cj
    return -2.0 * cj * cj / (total * total) * (ui - uj) * (vi - vj)


def gradient(cond_pad, prob_pad, adj_pad):
    ci = cond_pad[1:-1, 1:-1]
    ui = prob_pad[1:-1, 1:-1]
    vi = adj_pad[1:-1, 1:-1]
    out = edge_term(ci, cond_pad[2:, 1:-1], ui, prob_pad[2:, 1:-1], vi, adj_pad[2:, 1:-1])
    out = out + edge_term(ci, cond_pad[:-2, 1:-1], ui, prob_pad[:-2, 1:-1], vi, adj_pad[:-2, 1:-1])
    out = out + edge_term(ci, cond_pad[1:-1, 2:], ui, prob_pad[1:-1, 2:], vi, adj_pad[1:-1, 2:])
    out = out + edge_term(ci, cond_pad[1:-1, :-2], ui, prob_pad[1:-1, :-2], vi, adj_pad[1:-1, :-2])
    cx = jnp.pad(ci, ((0, 0), (0, 0), (1, 1)))
    ux = jnp.pad(ui, ((0, 0), (0, 0), (1, 1)))
    vx = jnp.pad(vi, ((0, 0), (0, 0), (1, 1)))
    out = out + edge_term(ci, cx[..., 2:], ui, ux[..., 2:], vi, vx[..., 2:])
    return out + edge_term(ci, cx[..., :-2], ui, ux[..., :-2], vi, vx[..., :-2])


def moments(r, v, av):
    return [jnp.sum(r * r), jnp.sum(r * v), jnp.sum(v * v), jnp.sum(v * av)]


def steps(m0, m1, m2, m3):
    a0 = m0 / m1
    new = a0 * a0 * m2 - m0
    grow = 1.0 + new / m0
    a1 = new / (grow * grow * m1 - 2.0 * grow * a0 * m2 + a0 * a0 * m3)
    return a0 + a1 * grow, -a1 * a0


def per_device(conduct, seeds, labels, start, cotangent):
    free = seeds.astype(jnp.float32)
    rhs = seed_pull * (seeds * labels).astype(jnp.float32)
    fields, widths = [conduct, start, cotangent, free, rhs], [3, 3, 2, 2, 2]
    fields = extend(fields, widths, GY, 0)
    cond, begin, cot, free, rhs = extend(fields, widths, GZ, 1)
    coeffs = coefficients(cond, free)
    resid = rhs - operate(begin, coeffs)
    near, mid = inner(coeffs, 1), inner(coeffs, 2)
    image, image_cot = operate(resid, near), operate(cot, near)
    second, second_cot = operate(image, mid), operate(image_cot, mid)
    line = jnp.stack(
        moments(resid[2:-2, 2:-2], image[1:-1, 1:-1], second)
        + moments(cot[2:-2, 2:-2], image_cot[1:-1, 1:-1], second_cot)
    )
    total = over_copies(over_copies(line, GZ), GY)
    on_r, on_v = steps(total[0], total[1], total[2], total[3])
    on_s, on_u = steps(total[4], total[5], total[6], total[7])
    prob_pad = begin[2:-2, 2:-2] + on_r * resid[1:-1, 1:-1] + on_v * image
    adj_pad = on_s * cot[1:-1, 1:-1] + on_u * image_cot
    grad_conduct = gradient(cond[2:-2, 2:-2], prob_pad, adj_pad)
    return prob_pad[1:-1, 1:-1], adj_pad[1:-1, 1:-1], grad_conduct


def solution(mesh):
    split = Mesh(mesh.devices.reshape(4, 4, 16, 2), ("gy_0", "gy_1", "gz_0", "gz_1"))
    spec = P(GY, GZ, None)
    return jax.shard_map(per_device, mesh=split, in_specs=(spec,) * 5, out_specs=(spec,) * 3, check_vma=False)
```

```python
import jax
import jax.numpy as jnp
from jax import lax
from jax.experimental import pallas as pl
from jax.experimental.pallas import tpu as pltpu
from jax.sharding import Mesh
from jax.sharding import PartitionSpec as P

GY = ("gy_0", "gy_1")
GZ = ("gz_0", "gz_1")

seed_pull = 4.0
screening = 0.05

ROWS, COLS, LANES = 16, 32, 128
FRAME = COLS + 8
WIDTHS = (3, 3, 2, 2, 2)
PLACES = (0, 3, 6, 8, 10)
MESSAGE = 12


def neighbours(last, first, axis):
    devices = lax.axis_size(axis)
    up = [(i, i + 1) for i in range(devices - 1)]
    return lax.ppermute(last, axis, up), lax.ppermute(first, axis, [(b, a) for a, b in up])


def over_copies(shard, axis):
    copies = jnp.broadcast_to(shard, (lax.axis_size(axis), *shard.shape))
    return jnp.sum(lax.all_to_all(copies, axis, split_axis=0, concat_axis=0, tiled=True), axis=0)


def recip_sum(first, second):
    return 1.0 / jnp.maximum(first + second, 1e-30)


def harmonic(first, second):
    return 2.0 * first * second * recip_sum(first, second)


def next_z(a):
    return pltpu.roll(a, FRAME - 1, 0)


def prev_z(a):
    return pltpu.roll(a, 1, 0)


def next_x(a):
    return pltpu.roll(a, LANES - 1, 1)


def prev_x(a):
    return pltpu.roll(a, 1, 1)


class Frame:
    def __init__(self, own, low, high, side):
        self.own, self.low, self.high, self.side = own, low, high, side

    def row(self, field, y):
        w, at = WIDTHS[field], PLACES[field]
        if y < 3:
            main = self.low[at + y - (3 - w)]
        elif y >= 3 + ROWS:
            main = self.high[at + y - 3 - ROWS]
        elif field < 3:
            main = self.own[field][y - 3]
        elif field == 3:
            main = self.own[3][y - 3].astype(jnp.float32)
        else:
            main = seed_pull * (self.own[3][y - 3] * self.own[4][y - 3]).astype(jnp.float32)
        return jnp.concatenate([main, self.side[field, y]], axis=0)


def moments_kernel(k, s, c, sd, lb, low, high, side, r_out, v_out, u_out, line_out, wx, wy, wz, res):
    frame = Frame((k, s, c, sd, lb), low, high, side)
    lane = lax.broadcasted_iota(jnp.int32, (FRAME, LANES), 1)
    inside_x = jnp.where(lane < LANES - 1, 1.0, 0.0)
    for y in range(3 + ROWS + 3):
        here = frame.row(0, y)
        wz[y] = harmonic(here, next_z(here))
        wx[y] = harmonic(here, next_x(here)) * inside_x
        if y < 3 + ROWS + 2:
            wy[y] = harmonic(here, frame.row(0, y + 1))

    def apply(row, y, diagonal):
        here = row(y)
        fz = wz[y] * (here - next_z(here))
        fx = wx[y] * (here - next_x(here))
        out = diagonal * here + fz - prev_z(fz) + fx - prev_x(fx)
        return out + wy[y] * (here - row(y + 1)) + wy[y - 1] * (here - row(y - 1))

    def diagonal(y):
        return seed_pull * frame.row(3, y) + screening

    for y in range(1, 21):
        res[y] = frame.row(4, y) - apply(lambda i: frame.row(1, i), y, diagonal(y))
    for y in range(2, 20):
        d = diagonal(y)
        v_out[y - 2] = apply(lambda i: res[i], y, d)
        u_out[y - 2] = apply(lambda i: frame.row(2, i), y, d)
        r_out[y - 2] = res[y]

    sums = [jnp.zeros((8, LANES), jnp.float32) for _ in range(8)]

    def fold(a):
        return a[0:8] + a[8:16] + a[16:24] + a[24:32]

    for y in range(3, 3 + ROWS):
        d = diagonal(y)[:COLS]
        for base, krylov0, krylov1 in ((0, lambda i: res[i], v_out), (4, lambda i: frame.row(2, i), u_out)):
            r, v = krylov0(y)[:COLS], krylov1[y - 2]
            dz, dx, dy = v - next_z(v), v - next_x(v), v - krylov1[y - 1]
            v = v[:COLS]
            energy = (wz[y] * dz * dz + wx[y] * dx * dx + wy[y] * dy * dy)[:COLS] + d * v * v
            for i, term in enumerate((r * r, r * v, v * v, energy)):
                sums[base + i] = sums[base + i] + fold(term)
    line = jnp.zeros((8, LANES), jnp.float32)
    at = lax.broadcasted_iota(jnp.int32, (8, LANES), 1)
    for i, total in enumerate(sums):
        line = line + jnp.where(at == i, jnp.sum(total, axis=1, keepdims=True), 0.0)
    line_out[...] = jnp.sum(line, axis=0, keepdims=True)


def steps(m0, m1, m2, m3):
    a0 = m0 / m1
    new = a0 * a0 * m2 - m0
    grow = 1.0 + new / m0
    a1 = new / (grow * grow * m1 - 2.0 * grow * a0 * m2 + a0 * a0 * m3)
    return a0 + a1 * grow, -a1 * a0


def finish_kernel(k, s, c, sd, lb, low, high, side, r, v, u, line, prob_out, adj_out, grad_out, p, q):
    frame = Frame((k, s, c, sd, lb), low, high, side)
    total = jnp.sum(line[...], axis=0)
    at = lax.broadcasted_iota(jnp.int32, (1, LANES), 1)
    m = [jnp.sum(jnp.where(at == i, total, 0.0), axis=1, keepdims=True) for i in range(8)]
    m = [jnp.broadcast_to(one, (1, LANES)) for one in m]
    on_r, on_v = steps(*m[:4])
    on_s, on_u = steps(*m[4:])
    lane = lax.broadcasted_iota(jnp.int32, (FRAME, LANES), 1)
    inside_x = jnp.where(lane < LANES - 1, 1.0, 0.0)
    for y in range(18):
        p[y] = frame.row(1, y + 2) + on_r * r[y] + on_v * v[y]
        q[y] = on_s * frame.row(2, y + 2) + on_u * u[y]
    above = None
    for y in range(17):
        kk, pp, qq = frame.row(0, y + 2), p[y], q[y]
        kn = frame.row(0, y + 3)
        share = recip_sum(kk, kn)
        product = -2.0 * (pp - p[y + 1]) * (qq - q[y + 1]) * share * share
        before, above = above, kk * kk * product
        if y == 0:
            continue
        out = before + kn * kn * product
        kn = next_z(kk)
        share = recip_sum(kk, kn)
        product = -2.0 * (pp - next_z(pp)) * (qq - next_z(qq)) * share * share
        out = out + kn * kn * product + prev_z(kk * kk * product)
        kn = next_x(kk)
        share = recip_sum(kk, kn)
        product = -2.0 * (pp - next_x(pp)) * (qq - next_x(qq)) * share * share * inside_x
        out = out + kn * kn * product + prev_x(kk * kk * product)
        grad_out[y - 1] = out[:COLS]
        prob_out[y - 1] = pp[:COLS]
        adj_out[y - 1] = qq[:COLS]


def per_device(conduct, seeds, labels, start, cotangent):
    free = seeds.astype(jnp.float32)
    rhs = seed_pull * (seeds * labels).astype(jnp.float32)
    fields = (conduct, start, cotangent, free, rhs)
    last = jnp.concatenate([f[ROWS - w :] for f, w in zip(fields, WIDTHS)], axis=0)
    first = jnp.concatenate([f[:w] for f, w in zip(fields, WIDTHS)], axis=0)
    low, high = neighbours(last, first, GY)

    def column(field, pick):
        f, w, at = fields[field], WIDTHS[field], PLACES[field]
        rows = jnp.concatenate([pick(low[at : at + w], w), pick(f, w), pick(high[at : at + w], w)], axis=0)
        return jnp.pad(rows, ((3 - w, 3 - w), (0, 0), (0, 0)))

    last = jnp.concatenate([column(i, lambda a, w: a[:, COLS - w :]) for i in range(5)], axis=1)
    first = jnp.concatenate([column(i, lambda a, w: a[:, :w]) for i in range(5)], axis=1)
    left, right = neighbours(last, first, GZ)
    side = jnp.stack(
        [
            jnp.concatenate(
                [right[:, at : at + w], jnp.zeros((ROWS + 6, 8 - 2 * w, LANES), jnp.float32), left[:, at : at + w]],
                axis=1,
            )
            for w, at in zip(WIDTHS, PLACES)
        ]
    )
    vmem = pl.BlockSpec(memory_space=pltpu.VMEM)
    f32 = lambda *shape: jax.ShapeDtypeStruct(shape, jnp.float32)
    params = pltpu.CompilerParams(vmem_limit_bytes=48 * 1024 * 1024)
    held = (conduct, start, cotangent, seeds, labels, low, high, side)
    r, v, u, line = pl.pallas_call(
        moments_kernel,
        out_shape=(f32(18, FRAME, LANES),) * 3 + (f32(1, LANES),),
        in_specs=[vmem] * 8,
        out_specs=(vmem,) * 4,
        scratch_shapes=[pltpu.VMEM((22, FRAME, LANES), jnp.float32)] * 4,
        compiler_params=params,
        name="moments",
    )(*held)
    part = over_copies(line, GZ)
    copies = jnp.broadcast_to(part, (lax.axis_size(GY), *part.shape))
    parts = lax.all_to_all(copies, GY, split_axis=0, concat_axis=0, tiled=True)
    return pl.pallas_call(
        finish_kernel,
        out_shape=(f32(ROWS, COLS, LANES),) * 3,
        in_specs=[vmem] * 12,
        out_specs=(vmem,) * 3,
        scratch_shapes=[pltpu.VMEM((18, FRAME, LANES), jnp.float32)] * 2,
        compiler_params=params,
        name="finish",
    )(*held, r, v, u, parts)


def solution(mesh):
    split = Mesh(mesh.devices.reshape(4, 4, 16, 2), ("gy_0", "gy_1", "gz_0", "gz_1"))
    spec = P(GY, GZ, None)
    return jax.shard_map(per_device, mesh=split, in_specs=(spec,) * 5, out_specs=(spec,) * 3, check_vma=False)
```

```python
import jax
import jax.numpy as jnp
from jax import lax
from jax.experimental import pallas as pl
from jax.experimental.pallas import tpu as pltpu
from jax.sharding import Mesh
from jax.sharding import PartitionSpec as P

GY = ("gy_0", "gy_1")
GZ = ("gz_0", "gz_1")

seed_pull = 4.0
screening = 0.05

ROWS, COLS, LANES = 16, 32, 128
TALL = 24
PARTS = 7
ROW_MESSAGE = PARTS * COLS + 8
COL_MESSAGE = PARTS * TALL


def swap(even_pairs, odd_pairs, axis):
    n = lax.axis_size(axis)

    def pairs(begin):
        return [p for i in range(begin, n - 1, 2) for p in ((i, i + 1), (i + 1, i))]

    return lax.ppermute(even_pairs, axis, pairs(0)), lax.ppermute(odd_pairs, axis, pairs(1))


def from_all(shard, axis):
    copies = jnp.broadcast_to(shard, (lax.axis_size(axis), *shard.shape))
    return lax.all_to_all(copies, axis, split_axis=0, concat_axis=0, tiled=True)


def recip_sum(first, second):
    return 1.0 / jnp.maximum(first + second, 1e-30)


def harmonic(first, second):
    return 2.0 * first * second * recip_sum(first, second)


def after(a, axis):
    return pltpu.roll(a, a.shape[axis] - 1, axis)


def before(a, axis):
    return pltpu.roll(a, 1, axis)


def below(shape, axis, limit):
    return jnp.where(lax.broadcasted_iota(jnp.int32, shape, axis) < limit, 1.0, 0.0)


def row(ref, y):
    return ref[pl.ds(y * COLS, COLS), :]


def column(ref, z, skip=0):
    return ref[pl.ds(skip * COLS + z, ROWS, stride=COLS), :]


def within(k):
    wx = harmonic(k, after(k, 1)) * below(k.shape, 1, LANES - 1)
    wz = harmonic(k, after(k, 0)) * below(k.shape, 0, COLS - 1)
    return wx, wz


def in_row(f, wx, wz, base):
    fx = wx * (f - after(f, 1))
    fz = wz * (f - after(f, 0))
    return base * f + fx - before(fx, 1) + fz - before(fz, 0)


def base_of(seeds):
    return seed_pull * seeds.astype(jnp.float32) + screening


def pull_of(seeds, labels):
    return seed_pull * (seeds * labels).astype(jnp.float32)


def pack_kernel(odd_ref, k, s, c, sd, lb, one_out, two_out, floats, ints, sems):
    running = []
    for end in range(2):
        at = end * (ROWS - 3) * COLS
        for i, field in enumerate((k, s, c)):
            running.append((field.at[pl.ds(at, 3 * COLS)], floats.at[i, pl.ds(end * 3 * COLS, 3 * COLS)]))
        for i, field in enumerate((sd, lb)):
            running.append((field.at[pl.ds(at, 3 * COLS)], ints.at[i, pl.ds(end * 3 * COLS, 3 * COLS)]))
    running = [pltpu.make_async_copy(src, dst, sems.at[i]) for i, (src, dst) in enumerate(running)]
    for one in running:
        one.start()
    for one in running:
        one.wait()
    for slot, out in enumerate((one_out, two_out)):
        first = odd_ref[0] if slot == 0 else 1 - odd_ref[0]
        places = [pl.multiple_of((first * i + (1 - first) * (5 - i)) * COLS, COLS) for i in range(3)]
        k0, k1, k2 = [floats[0, pl.ds(p, COLS)] for p in places]
        s0, s1, s2 = [floats[1, pl.ds(p, COLS)] for p in places]
        c0, c1, _ = [floats[2, pl.ds(p, COLS)] for p in places]
        seeds0, seeds1, _ = [ints[0, pl.ds(p, COLS)] for p in places]
        labels0, labels1, _ = [ints[1, pl.ds(p, COLS)] for p in places]
        (wx0, wz0), (wx1, wz1) = within(k0), within(k1)
        w01, w12 = harmonic(k0, k1), harmonic(k1, k2)
        base0, base1 = base_of(seeds0), base_of(seeds1)
        q0 = pull_of(seeds0, labels0) - (in_row(s0, wx0, wz0, base0) + w01 * (s0 - s1))
        q1 = pull_of(seeds1, labels1) - (in_row(s1, wx1, wz1, base1) + w01 * (s1 - s0) + w12 * (s1 - s2))
        image = in_row(q0, wx0, wz0, base0) + w01 * (q0 - q1)
        image_cot = in_row(c0, wx0, wz0, base0) + w01 * (c0 - c1)
        diagonal = base0 + wx0 + before(wx0, 1) + wz0 + before(wz0, 0) + w01
        for i, part in enumerate((k0, s0, c0, q0, image, image_cot, diagonal)):
            out[pl.ds(i * COLS, COLS), :] = part
        at = lax.broadcasted_iota(jnp.int32, (8, LANES), 0)
        corner = jnp.where(at == 0, k1[0:8], k1[COLS - 8 :])
        corner = jnp.where(at == 1, before(s1[0:8], 0), corner)
        out[pl.ds(PARTS * COLS, 8), :] = jnp.where(at == 6, after(s1[COLS - 8 :], 0), corner)


def block_kernel(k, s, c, sd, lb, wx_out, wy_out, wz_out, r_out, v_out, u_out):
    for y in range(ROWS):
        here = row(k, y)
        wx, wz = within(here)
        wx_out[pl.ds(y * COLS, COLS), :] = wx
        wz_out[pl.ds(y * COLS, COLS), :] = wz
        if y < ROWS - 1:
            wy_out[pl.ds(y * COLS, COLS), :] = harmonic(here, row(k, y + 1))
    def apply(read, y):
        f = read(y)
        out = in_row(f, row(wx_out, y), row(wz_out, y), base_of(row(sd, y)))
        if y < ROWS - 1:
            out = out + row(wy_out, y) * (f - read(y + 1))
        if y > 0:
            out = out + row(wy_out, y - 1) * (f - read(y - 1))
        return out

    for y in range(ROWS):
        r_out[pl.ds(y * COLS, COLS), :] = pull_of(row(sd, y), row(lb, y)) - apply(lambda i: row(s, i), y)
        u_out[pl.ds(y * COLS, COLS), :] = apply(lambda i: row(c, i), y)
    for y in range(ROWS):
        v_out[pl.ds(y * COLS, COLS), :] = apply(lambda i: row(r_out, i), y)


def tall(own, plus1, plus2, minus2, minus1):
    at = lax.broadcasted_iota(jnp.int32, (8, LANES), 0)
    tail = jnp.where(at == 0, plus1, jnp.where(at == 7, minus1, 0.0))
    if plus2 is not None:
        tail = jnp.where(at == 1, plus2, jnp.where(at == 6, minus2, tail))
    return jnp.concatenate([own, tail], axis=0)


def rows_kernel(odd_ref, one, two, k, s, c, sd, wx, wy, wz, r_in, v_in, u_in, r, v, u, rims_out, low_out, cols_out, one_out, two_out):
    odd_row, odd_col = odd_ref[0] == 1, odd_ref[1] == 1
    kept = pl.ds(COLS, ROWS * COLS)
    r[kept, :], v[kept, :], u[kept, :] = r_in[...], v_in[...], u_in[...]

    def arrived(up, at, size):
        first, second = one[pl.ds(at, size), :], two[pl.ds(at, size), :]
        return jnp.where(odd_row, second, first) if up else jnp.where(odd_row, first, second)

    outer, corners, edges, diagonals = [], [], [], []
    for up in (False, True):
        ko, so, co, qo, image, image_cot, diagonal = [arrived(up, i * COLS, COLS) for i in range(PARTS)]
        corners.append(arrived(up, PARTS * COLS, 8))
        y, inner, inner_edge, beyond = (ROWS - 1, ROWS - 2, ROWS - 2, ROWS) if up else (0, 1, 0, -1)
        here, w = lambda a: pl.ds((a + 1) * COLS, COLS), harmonic(ko, row(k, y))
        edges.append(w)
        outer.append((ko, so, co))
        diagonals.append(diagonal + w)
        change = w * (so - row(s, y))
        q = r[here(y), :] + change
        qo = qo - change
        r[here(y), :] = q
        r[here(beyond), :] = qo
        wxo, wzo = within(ko)
        change_o = -change
        spread = wxo * after(change_o, 1) + before(wxo * change_o, 1) + wzo * after(change_o, 0) + before(wzo * change_o, 0)
        v[here(beyond), :] = image + diagonal * change_o - spread + w * (qo - q)
        u[here(beyond), :] = image_cot + w * (co - row(c, y))
        own = in_row(change, row(wx, y), row(wz, y), base_of(row(sd, y))) + row(wy, inner_edge) * change
        v[here(y), :] = v[here(y), :] + own + w * (q - qo)
        v[here(inner), :] = v[here(inner), :] - row(wy, inner_edge) * change
        u[here(y), :] = u[here(y), :] + w * (row(c, y) - co)
    for i, part in enumerate(outer[0] + outer[1]):
        rims_out[pl.ds(i * COLS, COLS), :] = part
    low_out[...] = edges[0]

    sides = []
    for right in (False, True):
        z = COLS - 1 if right else 0
        zin = z - 1 if right else 1
        pick = lambda a, z=z: a[z : z + 1]
        ck, cs = (7, 6) if right else (0, 1)
        (kl, sl, cl), (kh, sh, ch) = outer
        kc = tall(column(k, z), pick(kh), corners[1][ck : ck + 1], corners[0][ck : ck + 1], pick(kl))
        sc = tall(column(s, z), pick(sh), corners[1][cs : cs + 1], corners[0][cs : cs + 1], pick(sl))
        cc = tall(column(c, z), pick(ch), None, None, pick(cl))
        kin = tall(column(k, zin), pick(kh, zin), None, None, pick(kl, zin))
        rc, vc, uc = (
            tall(column(f, z, 1), f[pl.ds((ROWS + 1) * COLS + z, 1), :], None, None, f[pl.ds(z, 1), :])
            for f in (r, v, u)
        )
        wxc = harmonic(kc, after(kc, 1)) * below(kc.shape, 1, LANES - 1)
        wyc = harmonic(kc, after(kc, 0))
        dc = wxc + before(wxc, 1) + wyc + before(wyc, 0) + harmonic(kc, kin)
        dc = tall(dc[:ROWS] + base_of(column(sd, z)), pick(diagonals[1]), None, None, pick(diagonals[0]))
        for i, part in enumerate((kc, sc, cc, dc, kin)):
            cols_out[pl.ds((5 * right + i) * TALL, TALL), :] = part
        sides.append((kc, sc, cc, rc, vc, uc, dc))
    for i, (first, last) in enumerate(zip(*sides)):
        one_out[pl.ds(i * TALL, TALL), :] = jnp.where(odd_col, first, last)
        two_out[pl.ds(i * TALL, TALL), :] = jnp.where(odd_col, last, first)


def inner_kernel(c, sd, wx, wy, wz, low, r, v, u, sums_out):
    at = lax.broadcasted_iota(jnp.int32, (COLS, LANES), 0)
    mask = jnp.where((at >= 2) & (at < COLS - 2), 1.0, 0.0)
    mask_z = jnp.where((at >= 2) & (at < COLS - 3), 1.0, 0.0)
    sums = [jnp.zeros((COLS, LANES), jnp.float32) for _ in range(8)]
    for y in range(ROWS):
        base = base_of(row(sd, y))
        wxy, wzy = row(wx, y) * mask, row(wz, y) * mask_z
        wyy = (row(wy, y - 1) if y else low[...]) * mask
        for i, first, second in ((0, row(r, y + 1), v), (4, row(c, y), u)):
            image, under = row(second, y + 1), row(second, y)
            dx, dz, dy = image - after(image, 1), image - after(image, 0), image - under
            kept, kept_first = image * mask, first * mask
            sums[i] = sums[i] + kept_first * first
            sums[i + 1] = sums[i + 1] + kept_first * image
            sums[i + 2] = sums[i + 2] + kept * image
            sums[i + 3] = sums[i + 3] + wxy * dx * dx + wzy * dz * dz + wyy * dy * dy + base * kept * image
    for i, total in enumerate(sums):
        sums_out[pl.ds(i * 8, 8), :] = total[0:8] + total[8:16] + total[16:24] + total[24:32]


def columns_kernel(odd_ref, one, two, cols, c, sd, wz, sums, r, v, u, side_out, line_out):
    odd_col = odd_ref[1] == 1
    totals = [sums[pl.ds(i * 8, 8), :] for i in range(8)]

    def get(ref, z):
        return tall(column(ref, z, 1), ref[pl.ds((ROWS + 1) * COLS + z, 1), :], None, None, ref[pl.ds(z, 1), :])

    def gather(base, wxc, wyc, pairs, z_edges):
        for i, (first, image, z_terms) in enumerate(zip((pairs[0], pairs[2]), (pairs[1], pairs[3]), z_edges)):
            dx, dy = image - after(image, 1), image - before(image, 0)
            energy = wxc * dx * dx + before(wyc, 0) * dy * dy
            own, energy = image[:ROWS], energy[:ROWS] + base * image[:ROWS] * image[:ROWS]
            for w, other in z_terms:
                dz = own - other[:ROWS]
                energy = energy + w[:ROWS] * dz * dz
            for j, term in enumerate((first * first, first * own, own * own, energy)):
                totals[4 * i + j] = totals[4 * i + j] + term[:8] + term[8:16]

    lanes = below((TALL, LANES), 1, LANES - 1)
    for right in (False, True):
        z, zin, zdeep = (COLS - 1, COLS - 2, COLS - 3) if right else (0, 1, 2)

        def arrived(i):
            first, second = one[pl.ds(i * TALL, TALL), :], two[pl.ds(i * TALL, TALL), :]
            return jnp.where(odd_col, second, first) if right else jnp.where(odd_col, first, second)

        ko, so, co, qo, image, image_cot, diagonal = [arrived(i) for i in range(PARTS)]
        kc, sc, cc, dc, kin = [cols[pl.ds((5 * right + i) * TALL, TALL), :] for i in range(5)]
        w = harmonic(ko, kc)
        win = harmonic(kc, kin)
        change = w * (so - sc)

        def spread(kk, f):
            wxk, wyk = harmonic(kk, after(kk, 1)) * lanes, harmonic(kk, after(kk, 0))
            return (
                wxk * after(f, 1) + before(wxk * f, 1) + wyk * after(f, 0) + before(wyk * f, 0),
                wxk,
                wyk,
            )

        q = get(r, z) + change
        qo = qo - change
        own, wxc, wyc = spread(kc, change)
        change_v = dc * change - own + w * (q - qo)
        change_in = -win * change
        change_u = w * (cc - co)
        vc, vin, uc = get(v, z) + change_v, get(v, zin) + change_in, get(u, z) + change_u
        uin = get(u, zin)
        other, _, _ = spread(ko, -change)
        vo = image - diagonal * change - other + w * (qo - q)
        uo = image_cot + w * (co - cc)
        for i, part in enumerate((ko, so, co, qo, vo, uo, change, change_v, change_in, change_u)):
            side_out[pl.ds((10 * right + i) * TALL, TALL), :] = part
        wdeep = column(wz, zdeep if right else zin)
        vdeep, udeep = column(v, zdeep, 1), column(u, zdeep, 1)
        outside = ([(w, vo)], [(w, uo)]) if right else ([], [])
        gather(
            base_of(column(sd, z)),
            wxc,
            wyc,
            (q[:ROWS], vc, cc[:ROWS], uc),
            (outside[0] + [(win, vin)], outside[1] + [(win, uin)]),
        )
        gather(
            base_of(column(sd, zin)),
            harmonic(kin, after(kin, 1)) * lanes,
            harmonic(kin, after(kin, 0)),
            (column(r, zin, 1), vin, column(c, zin), uin),
            ([(wdeep, vdeep)], [(wdeep, udeep)]),
        )
    line = jnp.zeros((8, LANES), jnp.float32)
    at = lax.broadcasted_iota(jnp.int32, (8, LANES), 1)
    for i, total in enumerate(totals):
        line = line + jnp.where(at == i, jnp.sum(total, axis=1, keepdims=True), 0.0)
    line_out[...] = jnp.sum(line, axis=0, keepdims=True)


def steps(m0, m1, m2, m3):
    a0 = m0 / m1
    new = a0 * a0 * m2 - m0
    grow = 1.0 + new / m0
    a1 = new / (grow * grow * m1 - 2.0 * grow * a0 * m2 + a0 * a0 * m3)
    return a0 + a1 * grow, -a1 * a0


def finish_kernel(k, s, c, rims, side, r, v, u, line, prob_out, adj_out, grad_out, p, q):
    total = jnp.sum(line[...], axis=0)
    at = lax.broadcasted_iota(jnp.int32, (1, LANES), 1)
    m = [jnp.sum(jnp.where(at == i, total, 0.0), axis=1, keepdims=True) for i in range(8)]
    m = [jnp.broadcast_to(one, (1, LANES)) for one in m]
    on_r, on_v = steps(*m[:4])
    on_s, on_u = steps(*m[4:])

    def rows(field, ref, y):
        if 0 <= y < ROWS:
            return row(ref, y)
        return row(rims, field + (3 if y > 0 else 0))

    for y in range(-1, ROWS + 1):
        here = pl.ds((y + 1) * COLS, COLS)
        p[here, :] = rows(1, s, y) + on_r * r[here, :] + on_v * v[here, :]
        q[here, :] = on_s * rows(2, c, y) + on_u * u[here, :]
    for right in (False, True):
        z = COLS - 1 if right else 0
        change, change_v, change_in, change_u = [side[pl.ds((10 * right + i) * TALL, TALL), :] for i in range(6, 10)]
        zin = z - 1 if right else 1
        for ref, col, value in (
            (p, z, on_r * change + on_v * change_v),
            (p, zin, on_v * change_in),
            (q, z, on_u * change_u),
        ):
            here = pl.ds(COLS + col, ROWS, stride=COLS)
            ref[here, :] = ref[here, :] + value[:ROWS]
            last = pl.ds((ROWS + 1) * COLS + col, 1)
            ref[last, :] = ref[last, :] + value[ROWS : ROWS + 1]
            ref[pl.ds(col, 1), :] = ref[pl.ds(col, 1), :] + value[TALL - 1 :]
    inside_x = below((COLS, LANES), 1, LANES - 1)
    inside_z = below((COLS, LANES), 0, COLS - 1)
    up = None
    for y in range(-1, ROWS):
        kk, pp, qq = rows(0, k, y), row(p, y + 1), row(q, y + 1)
        kn = rows(0, k, y + 1)
        share = recip_sum(kk, kn)
        product = -2.0 * (pp - row(p, y + 2)) * (qq - row(q, y + 2)) * share * share
        down, up = up, kk * kk * product
        if y < 0:
            continue
        out = down + kn * kn * product
        for axis, inside in ((0, inside_z), (1, inside_x)):
            kn = after(kk, axis)
            share = recip_sum(kk, kn)
            product = -2.0 * (pp - after(pp, axis)) * (qq - after(qq, axis)) * share * share * inside
            out = out + kn * kn * product + before(kk * kk * product, axis)
        here = pl.ds(y * COLS, COLS)
        grad_out[here, :] = out
        prob_out[here, :] = pp
        adj_out[here, :] = qq
    for right in (False, True):
        z = COLS - 1 if right else 0
        ko, so, co, ro, vo, uo = [side[pl.ds((10 * right + i) * TALL, ROWS), :] for i in range(6)]
        share = recip_sum(column(k, z), ko)
        po, qo = so + on_r * ro + on_v * vo, on_s * co + on_u * uo
        product = -2.0 * (column(p, z, 1) - po) * (column(q, z, 1) - qo) * share * share
        here = pl.ds(z, ROWS, stride=COLS)
        grad_out[here, :] = grad_out[here, :] + ko * ko * product


def per_device(*arguments):
    k, sd, lb, s, c = [a.reshape(ROWS * COLS, LANES) for a in arguments]
    vmem, smem = pl.BlockSpec(memory_space=pltpu.VMEM), pl.BlockSpec(memory_space=pltpu.SMEM)
    big = pltpu.CompilerParams(vmem_limit_bytes=40 * 1024 * 1024)

    def f32(*rows):
        return tuple(jax.ShapeDtypeStruct((n, LANES), jnp.float32) for n in rows)

    def cost(us):
        return pl.CostEstimate(flops=0, bytes_accessed=int(us * 3.0e6), transcendentals=0)

    odd = jnp.stack([lax.axis_index("gy_1") % 2, lax.axis_index("gz_1") % 2]).astype(jnp.int32)
    one, two = pl.pallas_call(
        pack_kernel,
        out_shape=f32(ROW_MESSAGE, ROW_MESSAGE),
        in_specs=[smem] + [pl.BlockSpec(memory_space=pl.ANY)] * 5,
        out_specs=(vmem,) * 2,
        scratch_shapes=[
            pltpu.VMEM((3, 6 * COLS, LANES), jnp.float32),
            pltpu.VMEM((2, 6 * COLS, LANES), jnp.int32),
            pltpu.SemaphoreType.DMA((10,)),
        ],
        compiler_params=pltpu.CompilerParams(vmem_limit_bytes=60 * 1024 * 1024),
        name="pack",
    )(odd, k, s, c, sd, lb)
    one, two = swap(one, two, GY)
    block, framed = ROWS * COLS, (ROWS + 2) * COLS
    wx, wy, wz, r, v, u = pl.pallas_call(
        block_kernel,
        out_shape=f32(*(block,) * 6),
        in_specs=[vmem] * 5,
        out_specs=(vmem,) * 6,
        compiler_params=big,
        cost_estimate=cost(2.0),
        name="block",
    )(k, s, c, sd, lb)
    r, v, u, rims, low, cols, zone, ztwo = pl.pallas_call(
        rows_kernel,
        out_shape=f32(framed, framed, framed, 6 * COLS, COLS, 10 * TALL, COL_MESSAGE, COL_MESSAGE),
        in_specs=[smem] + [vmem] * 12,
        out_specs=(vmem,) * 8,
        compiler_params=big,
        cost_estimate=cost(0.5),
        name="rows",
    )(odd, one, two, k, s, c, sd, wx, wy, wz, r, v, u)
    zone, ztwo = swap(zone, ztwo, GZ)
    (sums,) = pl.pallas_call(
        inner_kernel,
        out_shape=f32(64),
        in_specs=[vmem] * 9,
        out_specs=(vmem,),
        compiler_params=big,
        cost_estimate=cost(1.0),
        name="inner",
    )(c, sd, wx, wy, wz, low, r, v, u)
    side, line = pl.pallas_call(
        columns_kernel,
        out_shape=f32(20 * TALL, 1),
        in_specs=[smem] + [vmem] * 10,
        out_specs=(vmem,) * 2,
        compiler_params=big,
        cost_estimate=cost(0.5),
        name="columns",
    )(odd, zone, ztwo, cols, c, sd, wz, sums, r, v, u)
    parts = from_all(jnp.sum(from_all(line, GZ), axis=0), GY)
    outs = pl.pallas_call(
        finish_kernel,
        out_shape=f32(block, block, block),
        in_specs=[vmem] * 9,
        out_specs=(vmem,) * 3,
        scratch_shapes=[pltpu.VMEM((framed, LANES), jnp.float32)] * 2,
        compiler_params=big,
        name="finish",
    )(k, s, c, rims, side, r, v, u, parts)
    return tuple(a.reshape(ROWS, COLS, LANES) for a in outs)


def solution(mesh):
    split = Mesh(mesh.devices.reshape(4, 4, 16, 2), ("gy_0", "gy_1", "gz_0", "gz_1"))
    spec = P(GY, GZ, None)
    return jax.shard_map(per_device, mesh=split, in_specs=(spec,) * 5, out_specs=(spec,) * 3, check_vma=False)
```

```python
import jax
import jax.numpy as jnp
from jax import lax
from jax.experimental import pallas as pl
from jax.experimental.pallas import tpu as pltpu
from jax.sharding import Mesh
from jax.sharding import PartitionSpec as P

GY = ("gy_0", "gy_1")
GZ = ("gz_0", "gz_1")

seed_pull = 4.0
screening = 0.05

ROWS, COLS, LANES = 16, 32, 128
TALL = 24
PARTS = 7
ROW_MESSAGE = PARTS * COLS + 8
COL_MESSAGE = PARTS * TALL


def swap(even_pairs, odd_pairs, axis):
    n = lax.axis_size(axis)

    def pairs(begin):
        return [p for i in range(begin, n - 1, 2) for p in ((i, i + 1), (i + 1, i))]

    odd_pairs = lax.ppermute(odd_pairs, axis, pairs(1))
    return lax.ppermute(even_pairs, axis, pairs(0)), odd_pairs


def from_all(shard, axis):
    copies = jnp.broadcast_to(shard, (lax.axis_size(axis), *shard.shape))
    return lax.all_to_all(copies, axis, split_axis=0, concat_axis=0, tiled=True)


def recip_sum(first, second):
    return 1.0 / jnp.maximum(first + second, 1e-30)


def harmonic(first, second):
    return 2.0 * first * second * recip_sum(first, second)


def after(a, axis):
    return pltpu.roll(a, a.shape[axis] - 1, axis)


def before(a, axis):
    return pltpu.roll(a, 1, axis)


def below(shape, axis, limit):
    return jnp.where(lax.broadcasted_iota(jnp.int32, shape, axis) < limit, 1.0, 0.0)


def row(ref, y):
    return ref[pl.ds(y * COLS, COLS), :]


def column(ref, z, skip=0):
    return ref[pl.ds(skip * COLS + z, ROWS, stride=COLS), :]


def within(k):
    wx = harmonic(k, after(k, 1)) * below(k.shape, 1, LANES - 1)
    wz = harmonic(k, after(k, 0)) * below(k.shape, 0, COLS - 1)
    return wx, wz


def in_row(f, wx, wz, base):
    fx = wx * (f - after(f, 1))
    fz = wz * (f - after(f, 0))
    return base * f + fx - before(fx, 1) + fz - before(fz, 0)


def base_of(seeds):
    return seed_pull * seeds.astype(jnp.float32) + screening


def pull_of(seeds, labels):
    return seed_pull * (seeds * labels).astype(jnp.float32)


def is_odd(axis):
    return lax.rem(lax.axis_index(axis), 2) == 1


def pack_kernel(k, s, c, sd, lb, two_out, one_out, floats, ints, sems):
    odd_row = lax.rem(lax.axis_index("gy_1"), 2)
    running = []
    for end in range(2):
        at = end * (ROWS - 3) * COLS
        for i, field in enumerate((k, s, c)):
            running.append((field.at[pl.ds(at, 3 * COLS)], floats.at[i, pl.ds(end * 3 * COLS, 3 * COLS)]))
        for i, field in enumerate((sd, lb)):
            running.append((field.at[pl.ds(at, 3 * COLS)], ints.at[i, pl.ds(end * 3 * COLS, 3 * COLS)]))
    running = [pltpu.make_async_copy(src, dst, sems.at[i]) for i, (src, dst) in enumerate(running)]
    for one in running:
        one.start()
    for one in running:
        one.wait()
    for slot, out in enumerate((one_out, two_out)):
        first = odd_row if slot == 0 else 1 - odd_row
        places = [pl.multiple_of((first * i + (1 - first) * (5 - i)) * COLS, COLS) for i in range(3)]
        k0, k1, k2 = [floats[0, pl.ds(p, COLS)] for p in places]
        s0, s1, s2 = [floats[1, pl.ds(p, COLS)] for p in places]
        c0, c1, _ = [floats[2, pl.ds(p, COLS)] for p in places]
        seeds0, seeds1, _ = [ints[0, pl.ds(p, COLS)] for p in places]
        labels0, labels1, _ = [ints[1, pl.ds(p, COLS)] for p in places]
        (wx0, wz0), (wx1, wz1) = within(k0), within(k1)
        w01, w12 = harmonic(k0, k1), harmonic(k1, k2)
        base0, base1 = base_of(seeds0), base_of(seeds1)
        q0 = pull_of(seeds0, labels0) - (in_row(s0, wx0, wz0, base0) + w01 * (s0 - s1))
        q1 = pull_of(seeds1, labels1) - (in_row(s1, wx1, wz1, base1) + w01 * (s1 - s0) + w12 * (s1 - s2))
        image = in_row(q0, wx0, wz0, base0) + w01 * (q0 - q1)
        image_cot = in_row(c0, wx0, wz0, base0) + w01 * (c0 - c1)
        diagonal = base0 + wx0 + before(wx0, 1) + wz0 + before(wz0, 0) + w01
        for i, part in enumerate((k0, s0, c0, q0, image, image_cot, diagonal)):
            out[pl.ds(i * COLS, COLS), :] = part
        at = lax.broadcasted_iota(jnp.int32, (8, LANES), 0)
        corner = jnp.where(at == 0, k1[0:8], k1[COLS - 8 :])
        corner = jnp.where(at == 1, before(s1[0:8], 0), corner)
        out[pl.ds(PARTS * COLS, 8), :] = jnp.where(at == 6, after(s1[COLS - 8 :], 0), corner)


def block_kernel(k, s, c, sd, lb, wx_out, wy_out, wz_out, r_out, v_out, u_out):
    for y in range(ROWS):
        here = row(k, y)
        wx, wz = within(here)
        wx_out[pl.ds(y * COLS, COLS), :] = wx
        wz_out[pl.ds(y * COLS, COLS), :] = wz
        if y < ROWS - 1:
            wy_out[pl.ds(y * COLS, COLS), :] = harmonic(here, row(k, y + 1))
    def apply(read, y):
        f = read(y)
        out = in_row(f, row(wx_out, y), row(wz_out, y), base_of(row(sd, y)))
        if y < ROWS - 1:
            out = out + row(wy_out, y) * (f - read(y + 1))
        if y > 0:
            out = out + row(wy_out, y - 1) * (f - read(y - 1))
        return out

    for y in range(ROWS):
        r_out[pl.ds(y * COLS, COLS), :] = pull_of(row(sd, y), row(lb, y)) - apply(lambda i: row(s, i), y)
        u_out[pl.ds(y * COLS, COLS), :] = apply(lambda i: row(c, i), y)
    for y in range(ROWS):
        v_out[pl.ds(y * COLS, COLS), :] = apply(lambda i: row(r_out, i), y)


def tall(own, plus1, plus2, minus2, minus1):
    at = lax.broadcasted_iota(jnp.int32, (8, LANES), 0)
    tail = jnp.where(at == 0, plus1, jnp.where(at == 7, minus1, 0.0))
    if plus2 is not None:
        tail = jnp.where(at == 1, plus2, jnp.where(at == 6, minus2, tail))
    return jnp.concatenate([own, tail], axis=0)


def rows_kernel(two, one, k, s, c, sd, wx, wy, wz, r_in, v_in, u_in, r, v, u, rims_out, low_out, cols_out, two_out, one_out):
    odd_row, odd_col = is_odd("gy_1"), is_odd("gz_1")
    kept = pl.ds(COLS, ROWS * COLS)
    r[kept, :], v[kept, :], u[kept, :] = r_in[...], v_in[...], u_in[...]

    def arrived(up, at, size):
        first, second = one[pl.ds(at, size), :], two[pl.ds(at, size), :]
        return jnp.where(odd_row, second, first) if up else jnp.where(odd_row, first, second)

    outer, corners, edges, diagonals = [], [], [], []
    for up in (False, True):
        ko, so, co, qo, image, image_cot, diagonal = [arrived(up, i * COLS, COLS) for i in range(PARTS)]
        corners.append(arrived(up, PARTS * COLS, 8))
        y, inner, inner_edge, beyond = (ROWS - 1, ROWS - 2, ROWS - 2, ROWS) if up else (0, 1, 0, -1)
        here, w = lambda a: pl.ds((a + 1) * COLS, COLS), harmonic(ko, row(k, y))
        edges.append(w)
        outer.append((ko, so, co))
        diagonals.append(diagonal + w)
        change = w * (so - row(s, y))
        q = r[here(y), :] + change
        qo = qo - change
        r[here(y), :] = q
        r[here(beyond), :] = qo
        wxo, wzo = within(ko)
        change_o = -change
        spread = wxo * after(change_o, 1) + before(wxo * change_o, 1) + wzo * after(change_o, 0) + before(wzo * change_o, 0)
        v[here(beyond), :] = image + diagonal * change_o - spread + w * (qo - q)
        u[here(beyond), :] = image_cot + w * (co - row(c, y))
        own = in_row(change, row(wx, y), row(wz, y), base_of(row(sd, y))) + row(wy, inner_edge) * change
        v[here(y), :] = v[here(y), :] + own + w * (q - qo)
        v[here(inner), :] = v[here(inner), :] - row(wy, inner_edge) * change
        u[here(y), :] = u[here(y), :] + w * (row(c, y) - co)
    for i, part in enumerate(outer[0] + outer[1]):
        rims_out[pl.ds(i * COLS, COLS), :] = part
    low_out[...] = edges[0]

    sides = []
    for right in (False, True):
        z = COLS - 1 if right else 0
        zin = z - 1 if right else 1
        pick = lambda a, z=z: a[z : z + 1]
        ck, cs = (7, 6) if right else (0, 1)
        (kl, sl, cl), (kh, sh, ch) = outer
        kc = tall(column(k, z), pick(kh), corners[1][ck : ck + 1], corners[0][ck : ck + 1], pick(kl))
        sc = tall(column(s, z), pick(sh), corners[1][cs : cs + 1], corners[0][cs : cs + 1], pick(sl))
        cc = tall(column(c, z), pick(ch), None, None, pick(cl))
        kin = tall(column(k, zin), pick(kh, zin), None, None, pick(kl, zin))
        rc, vc, uc = (
            tall(column(f, z, 1), f[pl.ds((ROWS + 1) * COLS + z, 1), :], None, None, f[pl.ds(z, 1), :])
            for f in (r, v, u)
        )
        wxc = harmonic(kc, after(kc, 1)) * below(kc.shape, 1, LANES - 1)
        wyc = harmonic(kc, after(kc, 0))
        dc = wxc + before(wxc, 1) + wyc + before(wyc, 0) + harmonic(kc, kin)
        dc = tall(dc[:ROWS] + base_of(column(sd, z)), pick(diagonals[1]), None, None, pick(diagonals[0]))
        for i, part in enumerate((kc, sc, cc, dc, kin)):
            cols_out[pl.ds((5 * right + i) * TALL, TALL), :] = part
        sides.append((kc, sc, cc, rc, vc, uc, dc))
    for i, (first, last) in enumerate(zip(*sides)):
        one_out[pl.ds(i * TALL, TALL), :] = jnp.where(odd_col, first, last)
        two_out[pl.ds(i * TALL, TALL), :] = jnp.where(odd_col, last, first)


def inner_kernel(c, sd, wx, wy, wz, low, r, v, u, sums_out):
    at = lax.broadcasted_iota(jnp.int32, (COLS, LANES), 0)
    mask = jnp.where((at >= 2) & (at < COLS - 2), 1.0, 0.0)
    mask_z = jnp.where((at >= 2) & (at < COLS - 3), 1.0, 0.0)
    sums = [jnp.zeros((COLS, LANES), jnp.float32) for _ in range(8)]
    for y in range(ROWS):
        base = base_of(row(sd, y))
        wxy, wzy = row(wx, y) * mask, row(wz, y) * mask_z
        wyy = (row(wy, y - 1) if y else low[...]) * mask
        for i, first, second in ((0, row(r, y + 1), v), (4, row(c, y), u)):
            image, under = row(second, y + 1), row(second, y)
            dx, dz, dy = image - after(image, 1), image - after(image, 0), image - under
            kept, kept_first = image * mask, first * mask
            sums[i] = sums[i] + kept_first * first
            sums[i + 1] = sums[i + 1] + kept_first * image
            sums[i + 2] = sums[i + 2] + kept * image
            sums[i + 3] = sums[i + 3] + wxy * dx * dx + wzy * dz * dz + wyy * dy * dy + base * kept * image
    for i, total in enumerate(sums):
        sums_out[pl.ds(i * 8, 8), :] = total[0:8] + total[8:16] + total[16:24] + total[24:32]


def columns_kernel(two, one, cols, c, sd, wz, sums, r, v, u, side_out, line_out):
    odd_col = is_odd("gz_1")
    totals = [sums[pl.ds(i * 8, 8), :] for i in range(8)]

    def get(ref, z):
        return tall(column(ref, z, 1), ref[pl.ds((ROWS + 1) * COLS + z, 1), :], None, None, ref[pl.ds(z, 1), :])

    def gather(base, wxc, wyc, pairs, z_edges):
        for i, (first, image, z_terms) in enumerate(zip((pairs[0], pairs[2]), (pairs[1], pairs[3]), z_edges)):
            dx, dy = image - after(image, 1), image - before(image, 0)
            energy = wxc * dx * dx + before(wyc, 0) * dy * dy
            own, energy = image[:ROWS], energy[:ROWS] + base * image[:ROWS] * image[:ROWS]
            for w, other in z_terms:
                dz = own - other[:ROWS]
                energy = energy + w[:ROWS] * dz * dz
            for j, term in enumerate((first * first, first * own, own * own, energy)):
                totals[4 * i + j] = totals[4 * i + j] + term[:8] + term[8:16]

    lanes = below((TALL, LANES), 1, LANES - 1)
    for right in (False, True):
        z, zin, zdeep = (COLS - 1, COLS - 2, COLS - 3) if right else (0, 1, 2)

        def arrived(i):
            first, second = one[pl.ds(i * TALL, TALL), :], two[pl.ds(i * TALL, TALL), :]
            return jnp.where(odd_col, second, first) if right else jnp.where(odd_col, first, second)

        ko, so, co, qo, image, image_cot, diagonal = [arrived(i) for i in range(PARTS)]
        kc, sc, cc, dc, kin = [cols[pl.ds((5 * right + i) * TALL, TALL), :] for i in range(5)]
        w = harmonic(ko, kc)
        win = harmonic(kc, kin)
        change = w * (so - sc)

        def spread(kk, f):
            wxk, wyk = harmonic(kk, after(kk, 1)) * lanes, harmonic(kk, after(kk, 0))
            return (
                wxk * after(f, 1) + before(wxk * f, 1) + wyk * after(f, 0) + before(wyk * f, 0),
                wxk,
                wyk,
            )

        q = get(r, z) + change
        qo = qo - change
        own, wxc, wyc = spread(kc, change)
        change_v = dc * change - own + w * (q - qo)
        change_in = -win * change
        change_u = w * (cc - co)
        vc, vin, uc = get(v, z) + change_v, get(v, zin) + change_in, get(u, z) + change_u
        uin = get(u, zin)
        other, _, _ = spread(ko, -change)
        vo = image - diagonal * change - other + w * (qo - q)
        uo = image_cot + w * (co - cc)
        for i, part in enumerate((ko, so, co, qo, vo, uo, change, change_v, change_in, change_u)):
            side_out[pl.ds((10 * right + i) * TALL, TALL), :] = part
        wdeep = column(wz, zdeep if right else zin)
        vdeep, udeep = column(v, zdeep, 1), column(u, zdeep, 1)
        outside = ([(w, vo)], [(w, uo)]) if right else ([], [])
        gather(
            base_of(column(sd, z)),
            wxc,
            wyc,
            (q[:ROWS], vc, cc[:ROWS], uc),
            (outside[0] + [(win, vin)], outside[1] + [(win, uin)]),
        )
        gather(
            base_of(column(sd, zin)),
            harmonic(kin, after(kin, 1)) * lanes,
            harmonic(kin, after(kin, 0)),
            (column(r, zin, 1), vin, column(c, zin), uin),
            ([(wdeep, vdeep)], [(wdeep, udeep)]),
        )
    line = jnp.zeros((8, LANES), jnp.float32)
    at = lax.broadcasted_iota(jnp.int32, (8, LANES), 1)
    for i, total in enumerate(totals):
        line = line + jnp.where(at == i, jnp.sum(total, axis=1, keepdims=True), 0.0)
    line_out[...] = jnp.sum(line, axis=0, keepdims=True)


def steps(m0, m1, m2, m3):
    a0 = m0 / m1
    new = a0 * a0 * m2 - m0
    grow = 1.0 + new / m0
    a1 = new / (grow * grow * m1 - 2.0 * grow * a0 * m2 + a0 * a0 * m3)
    return a0 + a1 * grow, -a1 * a0


def finish_kernel(k, s, c, rims, side, r, v, u, line, prob_out, adj_out, grad_out, p, q):
    total = jnp.sum(line[...], axis=0)
    at = lax.broadcasted_iota(jnp.int32, (1, LANES), 1)
    m = [jnp.sum(jnp.where(at == i, total, 0.0), axis=1, keepdims=True) for i in range(8)]
    m = [jnp.broadcast_to(one, (1, LANES)) for one in m]
    on_r, on_v = steps(*m[:4])
    on_s, on_u = steps(*m[4:])

    def rows(field, ref, y):
        if 0 <= y < ROWS:
            return row(ref, y)
        return row(rims, field + (3 if y > 0 else 0))

    for y in range(-1, ROWS + 1):
        here = pl.ds((y + 1) * COLS, COLS)
        p[here, :] = rows(1, s, y) + on_r * r[here, :] + on_v * v[here, :]
        q[here, :] = on_s * rows(2, c, y) + on_u * u[here, :]
    for right in (False, True):
        z = COLS - 1 if right else 0
        change, change_v, change_in, change_u = [side[pl.ds((10 * right + i) * TALL, TALL), :] for i in range(6, 10)]
        zin = z - 1 if right else 1
        for ref, col, value in (
            (p, z, on_r * change + on_v * change_v),
            (p, zin, on_v * change_in),
            (q, z, on_u * change_u),
        ):
            here = pl.ds(COLS + col, ROWS, stride=COLS)
            ref[here, :] = ref[here, :] + value[:ROWS]
            last = pl.ds((ROWS + 1) * COLS + col, 1)
            ref[last, :] = ref[last, :] + value[ROWS : ROWS + 1]
            ref[pl.ds(col, 1), :] = ref[pl.ds(col, 1), :] + value[TALL - 1 :]
    inside_x = below((COLS, LANES), 1, LANES - 1)
    inside_z = below((COLS, LANES), 0, COLS - 1)
    up = None
    for y in range(-1, ROWS):
        kk, pp, qq = rows(0, k, y), row(p, y + 1), row(q, y + 1)
        kn = rows(0, k, y + 1)
        share = recip_sum(kk, kn)
        product = -2.0 * (pp - row(p, y + 2)) * (qq - row(q, y + 2)) * share * share
        down, up = up, kk * kk * product
        if y < 0:
            continue
        out = down + kn * kn * product
        for axis, inside in ((0, inside_z), (1, inside_x)):
            kn = after(kk, axis)
            share = recip_sum(kk, kn)
            product = -2.0 * (pp - after(pp, axis)) * (qq - after(qq, axis)) * share * share * inside
            out = out + kn * kn * product + before(kk * kk * product, axis)
        here = pl.ds(y * COLS, COLS)
        grad_out[here, :] = out
        prob_out[here, :] = pp
        adj_out[here, :] = qq
    for right in (False, True):
        z = COLS - 1 if right else 0
        ko, so, co, ro, vo, uo = [side[pl.ds((10 * right + i) * TALL, ROWS), :] for i in range(6)]
        share = recip_sum(column(k, z), ko)
        po, qo = so + on_r * ro + on_v * vo, on_s * co + on_u * uo
        product = -2.0 * (column(p, z, 1) - po) * (column(q, z, 1) - qo) * share * share
        here = pl.ds(z, ROWS, stride=COLS)
        grad_out[here, :] = grad_out[here, :] + ko * ko * product


def per_device(*arguments):
    k, sd, lb, s, c = [a.reshape(ROWS * COLS, LANES) for a in arguments]
    vmem = pl.BlockSpec(memory_space=pltpu.VMEM)
    big = pltpu.CompilerParams(vmem_limit_bytes=40 * 1024 * 1024)

    def f32(*rows):
        return tuple(jax.ShapeDtypeStruct((n, LANES), jnp.float32) for n in rows)

    def cost(us):
        return pl.CostEstimate(flops=0, bytes_accessed=int(us * 3.0e6), transcendentals=0)

    two, one = pl.pallas_call(
        pack_kernel,
        out_shape=f32(ROW_MESSAGE, ROW_MESSAGE),
        in_specs=[pl.BlockSpec(memory_space=pl.ANY)] * 5,
        out_specs=(vmem,) * 2,
        scratch_shapes=[
            pltpu.VMEM((3, 6 * COLS, LANES), jnp.float32),
            pltpu.VMEM((2, 6 * COLS, LANES), jnp.int32),
            pltpu.SemaphoreType.DMA((10,)),
        ],
        compiler_params=pltpu.CompilerParams(vmem_limit_bytes=60 * 1024 * 1024),
        name="pack",
    )(k, s, c, sd, lb)
    one, two = swap(one, two, GY)
    block, framed = ROWS * COLS, (ROWS + 2) * COLS
    wx, wy, wz, r, v, u = pl.pallas_call(
        block_kernel,
        out_shape=f32(*(block,) * 6),
        in_specs=[vmem] * 5,
        out_specs=(vmem,) * 6,
        compiler_params=big,
        cost_estimate=cost(2.0),
        name="block",
    )(k, s, c, sd, lb)
    r, v, u, rims, low, cols, ztwo, zone = pl.pallas_call(
        rows_kernel,
        out_shape=f32(framed, framed, framed, 6 * COLS, COLS, 10 * TALL, COL_MESSAGE, COL_MESSAGE),
        in_specs=[vmem] * 12,
        out_specs=(vmem,) * 8,
        compiler_params=big,
        cost_estimate=cost(0.5),
        name="rows",
    )(two, one, k, s, c, sd, wx, wy, wz, r, v, u)
    zone, ztwo = swap(zone, ztwo, GZ)
    (sums,) = pl.pallas_call(
        inner_kernel,
        out_shape=f32(64),
        in_specs=[vmem] * 9,
        out_specs=(vmem,),
        compiler_params=big,
        cost_estimate=cost(1.0),
        name="inner",
    )(c, sd, wx, wy, wz, low, r, v, u)
    side, line = pl.pallas_call(
        columns_kernel,
        out_shape=f32(20 * TALL, 1),
        in_specs=[vmem] * 10,
        out_specs=(vmem,) * 2,
        compiler_params=big,
        cost_estimate=cost(0.5),
        name="columns",
    )(ztwo, zone, cols, c, sd, wz, sums, r, v, u)
    parts = from_all(jnp.sum(from_all(line, GZ), axis=0), GY)
    outs = pl.pallas_call(
        finish_kernel,
        out_shape=f32(block, block, block),
        in_specs=[vmem] * 9,
        out_specs=(vmem,) * 3,
        scratch_shapes=[pltpu.VMEM((framed, LANES), jnp.float32)] * 2,
        compiler_params=big,
        name="finish",
    )(k, s, c, rims, side, r, v, u, parts)
    return tuple(a.reshape(ROWS, COLS, LANES) for a in outs)


def solution(mesh):
    split = Mesh(mesh.devices.reshape(4, 4, 16, 2), ("gy_0", "gy_1", "gz_0", "gz_1"))
    spec = P(GY, GZ, None)
    return jax.shard_map(per_device, mesh=split, in_specs=(spec,) * 5, out_specs=(spec,) * 3, check_vma=False)
```

```python
import jax
import jax.numpy as jnp
from jax import lax
from jax.experimental import pallas as pl
from jax.experimental.pallas import tpu as pltpu
from jax.sharding import Mesh
from jax.sharding import PartitionSpec as P

GY = ("gy_0", "gy_1")
GZ = ("gz_0", "gz_1")

seed_pull = 4.0
screening = 0.05

ROWS, COLS, LANES = 16, 32, 128
TALL = 24
PARTS = 7
ROW_MESSAGE = PARTS * COLS + 8
COL_MESSAGE = PARTS * TALL
CHUNK = 4


def swap(even_pairs, odd_pairs, axis):
    n = lax.axis_size(axis)

    def pairs(begin):
        return [p for i in range(begin, n - 1, 2) for p in ((i, i + 1), (i + 1, i))]

    odd_pairs = lax.ppermute(odd_pairs, axis, pairs(1))
    return lax.ppermute(even_pairs, axis, pairs(0)), odd_pairs


def from_all(shard, axis):
    copies = jnp.broadcast_to(shard, (lax.axis_size(axis), *shard.shape))
    return lax.all_to_all(copies, axis, split_axis=0, concat_axis=0, tiled=True)


def recip_sum(first, second):
    return 1.0 / jnp.maximum(first + second, 1e-30)


def harmonic(first, second):
    return 2.0 * first * second * recip_sum(first, second)


def after(a, axis):
    return pltpu.roll(a, a.shape[axis] - 1, axis)


def before(a, axis):
    return pltpu.roll(a, 1, axis)


def below(shape, axis, limit):
    return jnp.where(lax.broadcasted_iota(jnp.int32, shape, axis) < limit, 1.0, 0.0)


def row(ref, y):
    return ref[pl.ds(y * COLS, COLS), :]


def column(ref, z, skip=0):
    return ref[pl.ds(skip * COLS + z, ROWS, stride=COLS), :]


def within(k):
    wx = harmonic(k, after(k, 1)) * below(k.shape, 1, LANES - 1)
    wz = harmonic(k, after(k, 0)) * below(k.shape, 0, COLS - 1)
    return wx, wz


def in_row(f, wx, wz, base):
    fx = wx * (f - after(f, 1))
    fz = wz * (f - after(f, 0))
    return base * f + fx - before(fx, 1) + fz - before(fz, 0)


def base_of(seeds):
    return seed_pull * seeds.astype(jnp.float32) + screening


def pull_of(seeds, labels):
    return seed_pull * (seeds * labels).astype(jnp.float32)


def is_odd(axis):
    return lax.rem(lax.axis_index(axis), 2) == 1


def pack_kernel(k, s, c, sd, lb, two_out, one_out, floats, ints, sems):
    odd_row = lax.rem(lax.axis_index("gy_1"), 2)
    running = []
    for end in range(2):
        at = end * (ROWS - 3) * COLS
        for i, field in enumerate((k, s, c)):
            running.append((field.at[pl.ds(at, 3 * COLS)], floats.at[i, pl.ds(end * 3 * COLS, 3 * COLS)]))
        for i, field in enumerate((sd, lb)):
            running.append((field.at[pl.ds(at, 3 * COLS)], ints.at[i, pl.ds(end * 3 * COLS, 3 * COLS)]))
    running = [pltpu.make_async_copy(src, dst, sems.at[i]) for i, (src, dst) in enumerate(running)]
    for one in running:
        one.start()
    for one in running:
        one.wait()
    for slot, out in enumerate((one_out, two_out)):
        first = odd_row if slot == 0 else 1 - odd_row
        places = [pl.multiple_of((first * i + (1 - first) * (5 - i)) * COLS, COLS) for i in range(3)]
        k0, k1, k2 = [floats[0, pl.ds(p, COLS)] for p in places]
        s0, s1, s2 = [floats[1, pl.ds(p, COLS)] for p in places]
        c0, c1, _ = [floats[2, pl.ds(p, COLS)] for p in places]
        seeds0, seeds1, _ = [ints[0, pl.ds(p, COLS)] for p in places]
        labels0, labels1, _ = [ints[1, pl.ds(p, COLS)] for p in places]
        (wx0, wz0), (wx1, wz1) = within(k0), within(k1)
        w01, w12 = harmonic(k0, k1), harmonic(k1, k2)
        base0, base1 = base_of(seeds0), base_of(seeds1)
        q0 = pull_of(seeds0, labels0) - (in_row(s0, wx0, wz0, base0) + w01 * (s0 - s1))
        q1 = pull_of(seeds1, labels1) - (in_row(s1, wx1, wz1, base1) + w01 * (s1 - s0) + w12 * (s1 - s2))
        image = in_row(q0, wx0, wz0, base0) + w01 * (q0 - q1)
        image_cot = in_row(c0, wx0, wz0, base0) + w01 * (c0 - c1)
        diagonal = base0 + wx0 + before(wx0, 1) + wz0 + before(wz0, 0) + w01
        for i, part in enumerate((k0, s0, c0, q0, image, image_cot, diagonal)):
            out[pl.ds(i * COLS, COLS), :] = part
        at = lax.broadcasted_iota(jnp.int32, (8, LANES), 0)
        corner = jnp.where(at == 0, k1[0:8], k1[COLS - 8 :])
        corner = jnp.where(at == 1, before(s1[0:8], 0), corner)
        out[pl.ds(PARTS * COLS, 8), :] = jnp.where(at == 6, after(s1[COLS - 8 :], 0), corner)


def edge(here, there, inside=None):
    share = recip_sum(here, there)
    if inside is not None:
        share = share * inside
    return 2.0 * here * there * share, share


def block_kernel(*refs):
    far, (k, s, c, sd, wx_out, wy_out, wz_out, r_out, v_out, u_out, shares_out, lb, sems) = refs[:5], refs[5:]
    coming = [
        [
            pltpu.make_async_copy(a.at[pl.ds(at, CHUNK * COLS)], b.at[pl.ds(at, CHUNK * COLS)], sems.at[i, at // (CHUNK * COLS)])
            for at in range(0, ROWS * COLS, CHUNK * COLS)
        ]
        for i, (a, b) in enumerate(zip(far, (k, s, c, sd, lb)))
    ]
    for chunks in coming:
        for chunk in chunks:
            chunk.start()

    def need(y, *fields):
        if y < ROWS and y % CHUNK == 0:
            for i in fields:
                coming[i][y // CHUNK].wait()

    inside_x = below((COLS, LANES), 1, LANES - 1)
    inside_z = below((COLS, LANES), 0, COLS - 1)
    need(0, 0)
    for y in range(ROWS):
        need(y + 1, 0)
        here = row(k, y)
        edges = [
            (wx_out, edge(here, after(here, 1), inside_x)),
            (wz_out, edge(here, after(here, 0), inside_z)),
        ]
        if y < ROWS - 1:
            edges.append((wy_out, edge(here, row(k, y + 1))))
        for i, (out, (w, share)) in enumerate(edges):
            out[pl.ds(y * COLS, COLS), :] = w
            shares_out[pl.ds((i * ROWS + y) * COLS, COLS), :] = share

    def apply(read, y):
        f = read(y)
        out = in_row(f, row(wx_out, y), row(wz_out, y), base_of(row(sd, y)))
        if y < ROWS - 1:
            out = out + row(wy_out, y) * (f - read(y + 1))
        if y > 0:
            out = out + row(wy_out, y - 1) * (f - read(y - 1))
        return out

    need(0, 1, 2, 3, 4)
    for y in range(ROWS):
        need(y + 1, 1, 2, 3, 4)
        r_out[pl.ds(y * COLS, COLS), :] = pull_of(row(sd, y), row(lb, y)) - apply(lambda i: row(s, i), y)
        u_out[pl.ds(y * COLS, COLS), :] = apply(lambda i: row(c, i), y)
    for y in range(ROWS):
        v_out[pl.ds(y * COLS, COLS), :] = apply(lambda i: row(r_out, i), y)


def tall(own, plus1, plus2, minus2, minus1):
    at = lax.broadcasted_iota(jnp.int32, (8, LANES), 0)
    tail = jnp.where(at == 0, plus1, jnp.where(at == 7, minus1, 0.0))
    if plus2 is not None:
        tail = jnp.where(at == 1, plus2, jnp.where(at == 6, minus2, tail))
    return jnp.concatenate([own, tail], axis=0)


def rows_kernel(two, one, k, s, c, sd, wx, wy, wz, r_in, v_in, u_in, r, v, u, low_out, cols_out, two_out, one_out):
    odd_row, odd_col = is_odd("gy_1"), is_odd("gz_1")
    kept = pl.ds(COLS, ROWS * COLS)
    r[kept, :], v[kept, :], u[kept, :] = r_in[...], v_in[...], u_in[...]

    def arrived(up, at, size):
        first, second = one[pl.ds(at, size), :], two[pl.ds(at, size), :]
        return jnp.where(odd_row, second, first) if up else jnp.where(odd_row, first, second)

    outer, corners, edges, diagonals = [], [], [], []
    for up in (False, True):
        ko, so, co, qo, image, image_cot, diagonal = [arrived(up, i * COLS, COLS) for i in range(PARTS)]
        corners.append(arrived(up, PARTS * COLS, 8))
        y, inner, inner_edge, beyond = (ROWS - 1, ROWS - 2, ROWS - 2, ROWS) if up else (0, 1, 0, -1)
        here, w = lambda a: pl.ds((a + 1) * COLS, COLS), harmonic(ko, row(k, y))
        edges.append(w)
        outer.append((ko, so, co))
        diagonals.append(diagonal + w)
        change = w * (so - row(s, y))
        q = r[here(y), :] + change
        qo = qo - change
        r[here(y), :] = q
        r[here(beyond), :] = qo
        wxo, wzo = within(ko)
        change_o = -change
        spread = wxo * after(change_o, 1) + before(wxo * change_o, 1) + wzo * after(change_o, 0) + before(wzo * change_o, 0)
        v[here(beyond), :] = image + diagonal * change_o - spread + w * (qo - q)
        u[here(beyond), :] = image_cot + w * (co - row(c, y))
        own = in_row(change, row(wx, y), row(wz, y), base_of(row(sd, y))) + row(wy, inner_edge) * change
        v[here(y), :] = v[here(y), :] + own + w * (q - qo)
        v[here(inner), :] = v[here(inner), :] - row(wy, inner_edge) * change
        u[here(y), :] = u[here(y), :] + w * (row(c, y) - co)
    for i, part in enumerate(outer[0] + outer[1]):
        cols_out[pl.ds(10 * TALL + i * COLS, COLS), :] = part
    low_out[...] = edges[0]

    sides = []
    for right in (False, True):
        z = COLS - 1 if right else 0
        zin = z - 1 if right else 1
        pick = lambda a, z=z: a[z : z + 1]
        ck, cs = (7, 6) if right else (0, 1)
        (kl, sl, cl), (kh, sh, ch) = outer
        kc = tall(column(k, z), pick(kh), corners[1][ck : ck + 1], corners[0][ck : ck + 1], pick(kl))
        sc = tall(column(s, z), pick(sh), corners[1][cs : cs + 1], corners[0][cs : cs + 1], pick(sl))
        cc = tall(column(c, z), pick(ch), None, None, pick(cl))
        kin = tall(column(k, zin), pick(kh, zin), None, None, pick(kl, zin))
        rc, vc, uc = (
            tall(column(f, z, 1), f[pl.ds((ROWS + 1) * COLS + z, 1), :], None, None, f[pl.ds(z, 1), :])
            for f in (r, v, u)
        )
        wxc = harmonic(kc, after(kc, 1)) * below(kc.shape, 1, LANES - 1)
        wyc = harmonic(kc, after(kc, 0))
        dc = wxc + before(wxc, 1) + wyc + before(wyc, 0) + harmonic(kc, kin)
        dc = tall(dc[:ROWS] + base_of(column(sd, z)), pick(diagonals[1]), None, None, pick(diagonals[0]))
        for i, part in enumerate((kc, sc, cc, dc, kin)):
            cols_out[pl.ds((5 * right + i) * TALL, TALL), :] = part
        sides.append((kc, sc, cc, rc, vc, uc, dc))
    for i, (first, last) in enumerate(zip(*sides)):
        one_out[pl.ds(i * TALL, TALL), :] = jnp.where(odd_col, first, last)
        two_out[pl.ds(i * TALL, TALL), :] = jnp.where(odd_col, last, first)


def inner_kernel(c, sd, wx, wy, wz, low, r, v, u, sums_out):
    at = lax.broadcasted_iota(jnp.int32, (COLS, LANES), 0)
    mask = jnp.where((at >= 2) & (at < COLS - 2), 1.0, 0.0)
    mask_z = jnp.where((at >= 2) & (at < COLS - 3), 1.0, 0.0)
    sums = [jnp.zeros((COLS, LANES), jnp.float32) for _ in range(8)]
    for y in range(ROWS):
        base = base_of(row(sd, y))
        wxy, wzy = row(wx, y) * mask, row(wz, y) * mask_z
        wyy = (row(wy, y - 1) if y else low[...]) * mask
        for i, first, second in ((0, row(r, y + 1), v), (4, row(c, y), u)):
            image, under = row(second, y + 1), row(second, y)
            dx, dz, dy = image - after(image, 1), image - after(image, 0), image - under
            kept, kept_first = image * mask, first * mask
            sums[i] = sums[i] + kept_first * first
            sums[i + 1] = sums[i + 1] + kept_first * image
            sums[i + 2] = sums[i + 2] + kept * image
            sums[i + 3] = sums[i + 3] + wxy * dx * dx + wzy * dz * dz + wyy * dy * dy + base * kept * image
    for i, total in enumerate(sums):
        sums_out[pl.ds(i * 8, 8), :] = total[0:8] + total[8:16] + total[16:24] + total[24:32]


def columns_kernel(two, one, cols, c, sd, wz, sums, r, v, u, side_out, line_out):
    odd_col = is_odd("gz_1")
    totals = [sums[pl.ds(i * 8, 8), :] for i in range(8)]

    def get(ref, z):
        return tall(column(ref, z, 1), ref[pl.ds((ROWS + 1) * COLS + z, 1), :], None, None, ref[pl.ds(z, 1), :])

    def gather(base, wxc, wyc, pairs, z_edges):
        for i, (first, image, z_terms) in enumerate(zip((pairs[0], pairs[2]), (pairs[1], pairs[3]), z_edges)):
            dx, dy = image - after(image, 1), image - before(image, 0)
            energy = wxc * dx * dx + before(wyc, 0) * dy * dy
            own, energy = image[:ROWS], energy[:ROWS] + base * image[:ROWS] * image[:ROWS]
            for w, other in z_terms:
                dz = own - other[:ROWS]
                energy = energy + w[:ROWS] * dz * dz
            for j, term in enumerate((first * first, first * own, own * own, energy)):
                totals[4 * i + j] = totals[4 * i + j] + term[:8] + term[8:16]

    lanes = below((TALL, LANES), 1, LANES - 1)
    for right in (False, True):
        z, zin, zdeep = (COLS - 1, COLS - 2, COLS - 3) if right else (0, 1, 2)

        def arrived(i):
            first, second = one[pl.ds(i * TALL, TALL), :], two[pl.ds(i * TALL, TALL), :]
            return jnp.where(odd_col, second, first) if right else jnp.where(odd_col, first, second)

        ko, so, co, qo, image, image_cot, diagonal = [arrived(i) for i in range(PARTS)]
        kc, sc, cc, dc, kin = [cols[pl.ds((5 * right + i) * TALL, TALL), :] for i in range(5)]
        w = harmonic(ko, kc)
        win = harmonic(kc, kin)
        change = w * (so - sc)

        def spread(kk, f):
            wxk, wyk = harmonic(kk, after(kk, 1)) * lanes, harmonic(kk, after(kk, 0))
            return (
                wxk * after(f, 1) + before(wxk * f, 1) + wyk * after(f, 0) + before(wyk * f, 0),
                wxk,
                wyk,
            )

        q = get(r, z) + change
        qo = qo - change
        own, wxc, wyc = spread(kc, change)
        change_v = dc * change - own + w * (q - qo)
        change_in = -win * change
        change_u = w * (cc - co)
        vc, vin, uc = get(v, z) + change_v, get(v, zin) + change_in, get(u, z) + change_u
        uin = get(u, zin)
        other, _, _ = spread(ko, -change)
        vo = image - diagonal * change - other + w * (qo - q)
        uo = image_cot + w * (co - cc)
        for i, part in enumerate((ko, so, co, qo, vo, uo, change, change_v, change_in, change_u)):
            side_out[pl.ds((10 * right + i) * TALL, TALL), :] = part
        wdeep = column(wz, zdeep if right else zin)
        vdeep, udeep = column(v, zdeep, 1), column(u, zdeep, 1)
        outside = ([(w, vo)], [(w, uo)]) if right else ([], [])
        gather(
            base_of(column(sd, z)),
            wxc,
            wyc,
            (q[:ROWS], vc, cc[:ROWS], uc),
            (outside[0] + [(win, vin)], outside[1] + [(win, uin)]),
        )
        gather(
            base_of(column(sd, zin)),
            harmonic(kin, after(kin, 1)) * lanes,
            harmonic(kin, after(kin, 0)),
            (column(r, zin, 1), vin, column(c, zin), uin),
            ([(wdeep, vdeep)], [(wdeep, udeep)]),
        )
    line = jnp.zeros((8, LANES), jnp.float32)
    at = lax.broadcasted_iota(jnp.int32, (8, LANES), 1)
    for i, total in enumerate(totals):
        line = line + jnp.where(at == i, jnp.sum(total, axis=1, keepdims=True), 0.0)
    line_out[...] = jnp.sum(line, axis=0, keepdims=True)


def steps(m0, m1, m2, m3):
    a0 = m0 / m1
    new = a0 * a0 * m2 - m0
    grow = 1.0 + new / m0
    a1 = new / (grow * grow * m1 - 2.0 * grow * a0 * m2 + a0 * a0 * m3)
    return a0 + a1 * grow, -a1 * a0


def finish_kernel(k, s, c, shares, cols, side, r, v, u, line, prob_out, adj_out, grad_out, p, q, grad, sems):
    total = jnp.sum(line[...], axis=0)
    at = lax.broadcasted_iota(jnp.int32, (1, LANES), 1)
    m = [jnp.sum(jnp.where(at == i, total, 0.0), axis=1, keepdims=True) for i in range(8)]
    m = [jnp.broadcast_to(one, (1, LANES)) for one in m]
    on_r, on_v = steps(*m[:4])
    on_s, on_u = steps(*m[4:])

    def rows(field, ref, y):
        if 0 <= y < ROWS:
            return row(ref, y)
        return cols[pl.ds(10 * TALL + (field + (3 if y > 0 else 0)) * COLS, COLS), :]

    for y in range(-1, ROWS + 1):
        here = pl.ds((y + 1) * COLS, COLS)
        p[here, :] = rows(1, s, y) + on_r * r[here, :] + on_v * v[here, :]
        q[here, :] = on_s * rows(2, c, y) + on_u * u[here, :]
    for right in (False, True):
        z = COLS - 1 if right else 0
        change, change_v, change_in, change_u = [side[pl.ds((10 * right + i) * TALL, TALL), :] for i in range(6, 10)]
        zin = z - 1 if right else 1
        for ref, col, value in (
            (p, z, on_r * change + on_v * change_v),
            (p, zin, on_v * change_in),
            (q, z, on_u * change_u),
        ):
            here = pl.ds(COLS + col, ROWS, stride=COLS)
            ref[here, :] = ref[here, :] + value[:ROWS]
            last = pl.ds((ROWS + 1) * COLS + col, 1)
            ref[last, :] = ref[last, :] + value[ROWS : ROWS + 1]
            ref[pl.ds(col, 1), :] = ref[pl.ds(col, 1), :] + value[TALL - 1 :]
    own = pl.ds(COLS, ROWS * COLS)
    sent = [
        pltpu.make_async_copy(p.at[own], prob_out, sems.at[0]),
        pltpu.make_async_copy(q.at[own], adj_out, sems.at[1]),
    ]
    for copy in sent:
        copy.start()
    outer = []
    for right in (False, True):
        z = COLS - 1 if right else 0
        ko, so, co, ro, vo, uo = [side[pl.ds((10 * right + i) * TALL, ROWS), :] for i in range(6)]
        share = ko * recip_sum(column(k, z), ko)
        po, qo = so + on_r * ro + on_v * vo, on_s * co + on_u * uo
        outer.append(-2.0 * (column(p, z, 1) - po) * (column(q, z, 1) - qo) * share * share)

    def share_of(i, y):
        return shares[pl.ds((i * ROWS + y) * COLS, COLS), :]

    def gives(kk, kn, share, product):
        to_here, to_there = kn * share, kk * share
        return to_here * to_here * product, to_there * to_there * product

    up = None
    for y in range(-1, ROWS):
        kk, pp, qq = rows(0, k, y), row(p, y + 1), row(q, y + 1)
        kn = rows(0, k, y + 1)
        share = share_of(2, y) if 0 <= y < ROWS - 1 else recip_sum(kk, kn)
        here, there = gives(kk, kn, share, -2.0 * (pp - row(p, y + 2)) * (qq - row(q, y + 2)))
        down, up = up, there
        if y < 0:
            continue
        out = down + here
        for i, axis in ((0, 1), (1, 0)):
            product = -2.0 * (pp - after(pp, axis)) * (qq - after(qq, axis))
            here, there = gives(kk, after(kk, axis), share_of(i, y), product)
            out = out + here + before(there, axis)
        grad[pl.ds(y * COLS, COLS), :] = out
        if y % CHUNK == CHUNK - 1:
            at = y + 1 - CHUNK
            for z, value in zip((0, COLS - 1), outer):
                here = pl.ds(at * COLS + z, CHUNK, stride=COLS)
                grad[here, :] = grad[here, :] + value[at : at + CHUNK]
            here = pl.ds(at * COLS, CHUNK * COLS)
            sent.append(pltpu.make_async_copy(grad.at[here], grad_out.at[here], sems.at[2 + at // CHUNK]))
            sent[-1].start()
    for copy in sent:
        copy.wait()


def per_device(*arguments):
    k, sd, lb, s, c = [a.reshape(ROWS * COLS, LANES) for a in arguments]
    vmem = pl.BlockSpec(memory_space=pltpu.VMEM)
    big = pltpu.CompilerParams(vmem_limit_bytes=40 * 1024 * 1024)

    def f32(*rows):
        return tuple(jax.ShapeDtypeStruct((n, LANES), jnp.float32) for n in rows)

    def cost(us):
        return pl.CostEstimate(flops=0, bytes_accessed=int(us * 3.0e6), transcendentals=0)

    far = [pltpu.with_memory_space_constraint(a, pltpu.HBM) for a in (k, s, c, sd, lb)]
    two, one = pl.pallas_call(
        pack_kernel,
        out_shape=f32(ROW_MESSAGE, ROW_MESSAGE),
        in_specs=[pl.BlockSpec(memory_space=pltpu.HBM)] * 5,
        out_specs=(vmem,) * 2,
        scratch_shapes=[
            pltpu.VMEM((3, 6 * COLS, LANES), jnp.float32),
            pltpu.VMEM((2, 6 * COLS, LANES), jnp.int32),
            pltpu.SemaphoreType.DMA((10,)),
        ],
        compiler_params=pltpu.CompilerParams(vmem_limit_bytes=16 * 1024 * 1024),
        name="pack",
    )(*far)
    one, two = swap(one, two, GY)
    block, framed = ROWS * COLS, (ROWS + 2) * COLS
    k, s, c, sd, wx, wy, wz, r, v, u, shares = pl.pallas_call(
        block_kernel,
        out_shape=f32(*(block,) * 3) + (jax.ShapeDtypeStruct((block, LANES), jnp.int32),) + f32(*(block,) * 6, 3 * block),
        in_specs=[pl.BlockSpec(memory_space=pltpu.HBM)] * 5,
        out_specs=(vmem,) * 11,
        scratch_shapes=[pltpu.VMEM((block, LANES), jnp.int32), pltpu.SemaphoreType.DMA((5, ROWS // CHUNK))],
        compiler_params=big,
        cost_estimate=cost(3.0),
        name="block",
    )(*far)
    r, v, u, low, cols, ztwo, zone = pl.pallas_call(
        rows_kernel,
        out_shape=f32(framed, framed, framed, COLS, 10 * TALL + 6 * COLS, COL_MESSAGE, COL_MESSAGE),
        in_specs=[vmem] * 12,
        out_specs=(vmem,) * 7,
        compiler_params=big,
        cost_estimate=cost(0.5),
        name="rows",
    )(two, one, k, s, c, sd, wx, wy, wz, r, v, u)
    zone, ztwo = swap(zone, ztwo, GZ)
    (sums,) = pl.pallas_call(
        inner_kernel,
        out_shape=f32(64),
        in_specs=[vmem] * 9,
        out_specs=(vmem,),
        compiler_params=big,
        cost_estimate=cost(1.0),
        name="inner",
    )(c, sd, wx, wy, wz, low, r, v, u)
    side, line = pl.pallas_call(
        columns_kernel,
        out_shape=f32(20 * TALL, 1),
        in_specs=[vmem] * 10,
        out_specs=(vmem,) * 2,
        compiler_params=big,
        cost_estimate=cost(0.5),
        name="columns",
    )(ztwo, zone, cols, c, sd, wz, sums, r, v, u)
    parts = from_all(jnp.sum(from_all(line, GZ), axis=0), GY)
    outs = pl.pallas_call(
        finish_kernel,
        out_shape=f32(block, block, block),
        in_specs=[vmem] * 10,
        out_specs=(pl.BlockSpec(memory_space=pltpu.HBM),) * 3,
        scratch_shapes=[
            pltpu.VMEM((framed, LANES), jnp.float32),
            pltpu.VMEM((framed, LANES), jnp.float32),
            pltpu.VMEM((block, LANES), jnp.float32),
            pltpu.SemaphoreType.DMA((2 + ROWS // CHUNK,)),
        ],
        compiler_params=big,
        name="finish",
    )(k, s, c, shares, cols, side, r, v, u, parts)
    return tuple(a.reshape(ROWS, COLS, LANES) for a in outs)


def solution(mesh):
    split = Mesh(mesh.devices.reshape(4, 4, 16, 2), ("gy_0", "gy_1", "gz_0", "gz_1"))
    spec = P(GY, GZ, None)
    return jax.shard_map(per_device, mesh=split, in_specs=(spec,) * 5, out_specs=(spec,) * 3, check_vma=False)
```

```python
import jax
import jax.numpy as jnp
from jax import lax
from jax.experimental import pallas as pl
from jax.experimental.pallas import tpu as pltpu
from jax.sharding import Mesh
from jax.sharding import PartitionSpec as P

GY = ("gy_0", "gy_1")
GZ = ("gz_0", "gz_1")

seed_pull = 4.0
screening = 0.05

ROWS, COLS, LANES = 16, 32, 128
TALL = 24
PARTS = 7
ROW_MESSAGE = PARTS * COLS + 8
COL_MESSAGE = PARTS * ROWS + 16
CHUNK = 4


def swap(even_pairs, odd_pairs, axis):
    n = lax.axis_size(axis)

    def pairs(begin):
        return [p for i in range(begin, n - 1, 2) for p in ((i, i + 1), (i + 1, i))]

    odd_pairs = lax.ppermute(odd_pairs, axis, pairs(1))
    return lax.ppermute(even_pairs, axis, pairs(0)), odd_pairs


def from_all(shard, axis):
    copies = jnp.broadcast_to(shard, (lax.axis_size(axis), *shard.shape))
    return lax.all_to_all(copies, axis, split_axis=0, concat_axis=0, tiled=True)


def recip_sum(first, second):
    return 1.0 / jnp.maximum(first + second, 1e-30)


def harmonic(first, second):
    return 2.0 * first * second * recip_sum(first, second)


def after(a, axis):
    return pltpu.roll(a, a.shape[axis] - 1, axis)


def before(a, axis):
    return pltpu.roll(a, 1, axis)


def below(shape, axis, limit):
    return jnp.where(lax.broadcasted_iota(jnp.int32, shape, axis) < limit, 1.0, 0.0)


def row(ref, y):
    return ref[pl.ds(y * COLS, COLS), :]


def column(ref, z, skip=0):
    return ref[pl.ds(skip * COLS + z, ROWS, stride=COLS), :]


def within(k):
    wx = harmonic(k, after(k, 1)) * below(k.shape, 1, LANES - 1)
    wz = harmonic(k, after(k, 0)) * below(k.shape, 0, COLS - 1)
    return wx, wz


def in_row(f, wx, wz, base):
    fx = wx * (f - after(f, 1))
    fz = wz * (f - after(f, 0))
    return base * f + fx - before(fx, 1) + fz - before(fz, 0)


def base_of(seeds):
    return seed_pull * seeds.astype(jnp.float32) + screening


def pull_of(seeds, labels):
    return seed_pull * (seeds * labels).astype(jnp.float32)


def is_odd(axis):
    return lax.rem(lax.axis_index(axis), 2) == 1


def pack_kernel(k, s, c, sd, lb, two_out, one_out, floats, ints, sems):
    odd_row = lax.rem(lax.axis_index("gy_1"), 2)
    running = []
    for end in range(2):
        at = end * (ROWS - 3) * COLS
        for i, field in enumerate((k, s, c)):
            running.append((field.at[pl.ds(at, 3 * COLS)], floats.at[i, pl.ds(end * 3 * COLS, 3 * COLS)]))
        for i, field in enumerate((sd, lb)):
            running.append((field.at[pl.ds(at, 3 * COLS)], ints.at[i, pl.ds(end * 3 * COLS, 3 * COLS)]))
    running = [pltpu.make_async_copy(src, dst, sems.at[i]) for i, (src, dst) in enumerate(running)]
    for one in running:
        one.start()
    for one in running:
        one.wait()
    for slot, out in enumerate((one_out, two_out)):
        first = odd_row if slot == 0 else 1 - odd_row
        places = [pl.multiple_of((first * i + (1 - first) * (5 - i)) * COLS, COLS) for i in range(3)]
        k0, k1, k2 = [floats[0, pl.ds(p, COLS)] for p in places]
        s0, s1, s2 = [floats[1, pl.ds(p, COLS)] for p in places]
        c0, c1, _ = [floats[2, pl.ds(p, COLS)] for p in places]
        seeds0, seeds1, _ = [ints[0, pl.ds(p, COLS)] for p in places]
        labels0, labels1, _ = [ints[1, pl.ds(p, COLS)] for p in places]
        (wx0, wz0), (wx1, wz1) = within(k0), within(k1)
        w01, w12 = harmonic(k0, k1), harmonic(k1, k2)
        base0, base1 = base_of(seeds0), base_of(seeds1)
        q0 = pull_of(seeds0, labels0) - (in_row(s0, wx0, wz0, base0) + w01 * (s0 - s1))
        q1 = pull_of(seeds1, labels1) - (in_row(s1, wx1, wz1, base1) + w01 * (s1 - s0) + w12 * (s1 - s2))
        image = in_row(q0, wx0, wz0, base0) + w01 * (q0 - q1)
        image_cot = in_row(c0, wx0, wz0, base0) + w01 * (c0 - c1)
        diagonal = base0 + wx0 + before(wx0, 1) + wz0 + before(wz0, 0) + w01
        for i, part in enumerate((k0, s0, c0, q0, image, image_cot, diagonal)):
            out[pl.ds(i * COLS, COLS), :] = part
        at = lax.broadcasted_iota(jnp.int32, (8, LANES), 0)
        corner = jnp.where(at == 0, k1[0:8], k1[COLS - 8 :])
        corner = jnp.where(at == 1, before(s1[0:8], 0), corner)
        out[pl.ds(PARTS * COLS, 8), :] = jnp.where(at == 6, after(s1[COLS - 8 :], 0), corner)


def edge(here, there, inside=None):
    share = there * recip_sum(here, there)
    if inside is not None:
        share = share * inside
    return 2.0 * here * share, share


def block_kernel(*refs):
    far, (k, s, c, sd, wx_out, wy_out, wz_out, r_out, v_out, u_out, shares_out, lb, sems) = refs[:5], refs[5:]
    coming = [
        [
            pltpu.make_async_copy(a.at[pl.ds(at, CHUNK * COLS)], b.at[pl.ds(at, CHUNK * COLS)], sems.at[i, at // (CHUNK * COLS)])
            for at in range(0, ROWS * COLS, CHUNK * COLS)
        ]
        for i, (a, b) in enumerate(zip(far, (k, s, c, sd, lb)))
    ]
    for chunks in coming:
        for chunk in chunks:
            chunk.start()

    def need(y, *fields):
        if y < ROWS and y % CHUNK == 0:
            for i in fields:
                coming[i][y // CHUNK].wait()

    inside_x = below((COLS, LANES), 1, LANES - 1)
    inside_z = below((COLS, LANES), 0, COLS - 1)
    need(0, 0)
    for y in range(ROWS):
        need(y + 1, 0)
        here = row(k, y)
        edges = [
            (wx_out, edge(here, after(here, 1), inside_x)),
            (wz_out, edge(here, after(here, 0), inside_z)),
        ]
        if y < ROWS - 1:
            edges.append((wy_out, edge(here, row(k, y + 1))))
        for i, (out, (w, share)) in enumerate(edges):
            out[pl.ds(y * COLS, COLS), :] = w
            shares_out[pl.ds((i * ROWS + y) * COLS, COLS), :] = share

    def apply(read, y):
        f = read(y)
        out = in_row(f, row(wx_out, y), row(wz_out, y), base_of(row(sd, y)))
        if y < ROWS - 1:
            out = out + row(wy_out, y) * (f - read(y + 1))
        if y > 0:
            out = out + row(wy_out, y - 1) * (f - read(y - 1))
        return out

    need(0, 1, 2, 3, 4)
    for y in range(ROWS):
        need(y + 1, 1, 2, 3, 4)
        r_out[pl.ds(y * COLS, COLS), :] = pull_of(row(sd, y), row(lb, y)) - apply(lambda i: row(s, i), y)
        u_out[pl.ds(y * COLS, COLS), :] = apply(lambda i: row(c, i), y)
    for y in range(ROWS):
        v_out[pl.ds(y * COLS, COLS), :] = apply(lambda i: row(r_out, i), y)


def tall(own, plus1, plus2, minus2, minus1):
    at = lax.broadcasted_iota(jnp.int32, (8, LANES), 0)
    tail = jnp.where(at == 0, plus1, jnp.where(at == 7, minus1, 0.0))
    if plus2 is not None:
        tail = jnp.where(at == 1, plus2, jnp.where(at == 6, minus2, tail))
    return jnp.concatenate([own, tail], axis=0)


def tail_rows(wide):
    at = lax.broadcasted_iota(jnp.int32, (8, LANES), 0)
    return (at < 2) | (at > 5) if wide else (at < 1) | (at > 6)


def tails_packed(k, s, c, q):
    return [jnp.where(tail_rows(True), k, pltpu.roll(s, 4, 0)), jnp.where(tail_rows(False), c, pltpu.roll(q, 4, 0))]


def tails_unpacked(k_s, c_q):
    pairs = ((k_s, True), (pltpu.roll(k_s, 4, 0), True), (c_q, False), (pltpu.roll(c_q, 4, 0), False))
    return [jnp.where(tail_rows(wide), a, 0.0) for a, wide in pairs]


def rows_kernel(two, one, k, s, c, sd, wx, wy, wz, r_in, v_in, u_in, r, v, u, low_out, cols_out, two_out, one_out):
    odd_row, odd_col = is_odd("gy_1"), is_odd("gz_1")
    kept = pl.ds(COLS, ROWS * COLS)
    r[kept, :], v[kept, :], u[kept, :] = r_in[...], v_in[...], u_in[...]

    def arrived(up, at, size):
        first, second = one[pl.ds(at, size), :], two[pl.ds(at, size), :]
        return jnp.where(odd_row, second, first) if up else jnp.where(odd_row, first, second)

    outer, corners, edges, diagonals = [], [], [], []
    for up in (False, True):
        ko, so, co, qo, image, image_cot, diagonal = [arrived(up, i * COLS, COLS) for i in range(PARTS)]
        corners.append(arrived(up, PARTS * COLS, 8))
        y, inner, inner_edge, beyond = (ROWS - 1, ROWS - 2, ROWS - 2, ROWS) if up else (0, 1, 0, -1)
        here, w = lambda a: pl.ds((a + 1) * COLS, COLS), harmonic(ko, row(k, y))
        edges.append(w)
        outer.append((ko, so, co))
        diagonals.append(diagonal + w)
        change = w * (so - row(s, y))
        q = r[here(y), :] + change
        qo = qo - change
        r[here(y), :] = q
        r[here(beyond), :] = qo
        wxo, wzo = within(ko)
        change_o = -change
        spread = wxo * after(change_o, 1) + before(wxo * change_o, 1) + wzo * after(change_o, 0) + before(wzo * change_o, 0)
        v[here(beyond), :] = image + diagonal * change_o - spread + w * (qo - q)
        u[here(beyond), :] = image_cot + w * (co - row(c, y))
        own = in_row(change, row(wx, y), row(wz, y), base_of(row(sd, y))) + row(wy, inner_edge) * change
        v[here(y), :] = v[here(y), :] + own + w * (q - qo)
        v[here(inner), :] = v[here(inner), :] - row(wy, inner_edge) * change
        u[here(y), :] = u[here(y), :] + w * (row(c, y) - co)
    for i, part in enumerate(outer[0] + outer[1]):
        cols_out[pl.ds(10 * TALL + i * COLS, COLS), :] = part
    low_out[...] = edges[0]

    sides = []
    for right in (False, True):
        z = COLS - 1 if right else 0
        zin = z - 1 if right else 1
        pick = lambda a, z=z: a[z : z + 1]
        ck, cs = (7, 6) if right else (0, 1)
        (kl, sl, cl), (kh, sh, ch) = outer
        kc = tall(column(k, z), pick(kh), corners[1][ck : ck + 1], corners[0][ck : ck + 1], pick(kl))
        sc = tall(column(s, z), pick(sh), corners[1][cs : cs + 1], corners[0][cs : cs + 1], pick(sl))
        cc = tall(column(c, z), pick(ch), None, None, pick(cl))
        kin = tall(column(k, zin), pick(kh, zin), None, None, pick(kl, zin))
        rc, vc, uc = (
            tall(column(f, z, 1), f[pl.ds((ROWS + 1) * COLS + z, 1), :], None, None, f[pl.ds(z, 1), :])
            for f in (r, v, u)
        )
        wxc = harmonic(kc, after(kc, 1)) * below(kc.shape, 1, LANES - 1)
        wyc = harmonic(kc, after(kc, 0))
        dc = wxc + before(wxc, 1) + wyc + before(wyc, 0) + harmonic(kc, kin)
        dc = tall(dc[:ROWS] + base_of(column(sd, z)), pick(diagonals[1]), None, None, pick(diagonals[0]))
        for i, part in enumerate((kc, sc, cc, dc, kin)):
            cols_out[pl.ds((5 * right + i) * TALL, TALL), :] = part
        sides.append((kc, sc, cc, rc, vc, uc, dc))
    packed = [[part[:ROWS] for part in side] + tails_packed(*(part[ROWS:] for part in side[:4])) for side in sides]
    at = 0
    for first, last in zip(*packed):
        here = pl.ds(at, first.shape[0])
        one_out[here, :] = jnp.where(odd_col, first, last)
        two_out[here, :] = jnp.where(odd_col, last, first)
        at += first.shape[0]


def inner_kernel(c, sd, wx, wy, wz, low, r, v, u, sums_out):
    at = lax.broadcasted_iota(jnp.int32, (COLS, LANES), 0)
    mask = jnp.where((at >= 2) & (at < COLS - 2), 1.0, 0.0)
    mask_z = jnp.where((at >= 2) & (at < COLS - 3), 1.0, 0.0)
    sums = [jnp.zeros((COLS, LANES), jnp.float32) for _ in range(8)]
    for y in range(ROWS):
        base = base_of(row(sd, y))
        wxy, wzy = row(wx, y) * mask, row(wz, y) * mask_z
        wyy = (row(wy, y - 1) if y else low[...]) * mask
        for i, first, second in ((0, row(r, y + 1), v), (4, row(c, y), u)):
            image, under = row(second, y + 1), row(second, y)
            dx, dz, dy = image - after(image, 1), image - after(image, 0), image - under
            kept, kept_first = image * mask, first * mask
            sums[i] = sums[i] + kept_first * first
            sums[i + 1] = sums[i + 1] + kept_first * image
            sums[i + 2] = sums[i + 2] + kept * image
            sums[i + 3] = sums[i + 3] + wxy * dx * dx + wzy * dz * dz + wyy * dy * dy + base * kept * image
    for i, total in enumerate(sums):
        sums_out[pl.ds(i * 8, 8), :] = total[0:8] + total[8:16] + total[16:24] + total[24:32]


def columns_kernel(two, one, cols, c, sd, wz, sums, r, v, u, side_out, line_out):
    odd_col = is_odd("gz_1")
    totals = [sums[pl.ds(i * 8, 8), :] for i in range(8)]

    def get(ref, z):
        return tall(column(ref, z, 1), ref[pl.ds((ROWS + 1) * COLS + z, 1), :], None, None, ref[pl.ds(z, 1), :])

    def gather(base, wxc, wyc, pairs, z_edges):
        for i, (first, image, z_terms) in enumerate(zip((pairs[0], pairs[2]), (pairs[1], pairs[3]), z_edges)):
            dx, dy = image - after(image, 1), image - before(image, 0)
            energy = wxc * dx * dx + before(wyc, 0) * dy * dy
            own, energy = image[:ROWS], energy[:ROWS] + base * image[:ROWS] * image[:ROWS]
            for w, other in z_terms:
                dz = own - other[:ROWS]
                energy = energy + w[:ROWS] * dz * dz
            for j, term in enumerate((first * first, first * own, own * own, energy)):
                totals[4 * i + j] = totals[4 * i + j] + term[:8] + term[8:16]

    lanes = below((TALL, LANES), 1, LANES - 1)
    for right in (False, True):
        z, zin, zdeep = (COLS - 1, COLS - 2, COLS - 3) if right else (0, 1, 2)

        def arrived(at, size):
            first, second = one[pl.ds(at, size), :], two[pl.ds(at, size), :]
            return jnp.where(odd_col, second, first) if right else jnp.where(odd_col, first, second)

        tails = tails_unpacked(*(arrived(PARTS * ROWS + at, 8) for at in (0, 8))) + [jnp.zeros((8, LANES), jnp.float32)] * 3
        ko, so, co, qo, image, image_cot, diagonal = [
            jnp.concatenate([arrived(i * ROWS, ROWS), tail], axis=0) for i, tail in enumerate(tails)
        ]
        kc, sc, cc, dc, kin = [cols[pl.ds((5 * right + i) * TALL, TALL), :] for i in range(5)]
        w = harmonic(ko, kc)
        win = harmonic(kc, kin)
        change = w * (so - sc)

        def spread(kk, f):
            wxk, wyk = harmonic(kk, after(kk, 1)) * lanes, harmonic(kk, after(kk, 0))
            return (
                wxk * after(f, 1) + before(wxk * f, 1) + wyk * after(f, 0) + before(wyk * f, 0),
                wxk,
                wyk,
            )

        q = get(r, z) + change
        qo = qo - change
        own, wxc, wyc = spread(kc, change)
        change_v = dc * change - own + w * (q - qo)
        change_in = -win * change
        change_u = w * (cc - co)
        vc, vin, uc = get(v, z) + change_v, get(v, zin) + change_in, get(u, z) + change_u
        uin = get(u, zin)
        other, _, _ = spread(ko, -change)
        vo = image - diagonal * change - other + w * (qo - q)
        uo = image_cot + w * (co - cc)
        for i, part in enumerate((ko, so, co, qo, vo, uo, change, change_v, change_in, change_u)):
            side_out[pl.ds((10 * right + i) * TALL, TALL), :] = part
        wdeep = column(wz, zdeep if right else zin)
        vdeep, udeep = column(v, zdeep, 1), column(u, zdeep, 1)
        outside = ([(w, vo)], [(w, uo)]) if right else ([], [])
        gather(
            base_of(column(sd, z)),
            wxc,
            wyc,
            (q[:ROWS], vc, cc[:ROWS], uc),
            (outside[0] + [(win, vin)], outside[1] + [(win, uin)]),
        )
        gather(
            base_of(column(sd, zin)),
            harmonic(kin, after(kin, 1)) * lanes,
            harmonic(kin, after(kin, 0)),
            (column(r, zin, 1), vin, column(c, zin), uin),
            ([(wdeep, vdeep)], [(wdeep, udeep)]),
        )
    line = jnp.zeros((8, LANES), jnp.float32)
    at = lax.broadcasted_iota(jnp.int32, (8, LANES), 1)
    for i, total in enumerate(totals):
        line = line + jnp.where(at == i, jnp.sum(total, axis=1, keepdims=True), 0.0)
    line_out[...] = jnp.sum(line, axis=0, keepdims=True)


def steps(m0, m1, m2, m3):
    a0 = m0 / m1
    new = a0 * a0 * m2 - m0
    grow = 1.0 + new / m0
    a1 = new / (grow * grow * m1 - 2.0 * grow * a0 * m2 + a0 * a0 * m3)
    return a0 + a1 * grow, -a1 * a0


def finish_kernel(k, s, c, shares, cols, side, r, v, u, line, prob_out, adj_out, grad_out, p, q, grad, sems):
    total = jnp.sum(line[...], axis=0)
    at = lax.broadcasted_iota(jnp.int32, (1, LANES), 1)
    m = [jnp.sum(jnp.where(at == i, total, 0.0), axis=1, keepdims=True) for i in range(8)]
    m = [jnp.broadcast_to(one, (1, LANES)) for one in m]
    on_r, on_v = steps(*m[:4])
    on_s, on_u = steps(*m[4:])

    def rows(field, ref, y):
        if 0 <= y < ROWS:
            return row(ref, y)
        return cols[pl.ds(10 * TALL + (field + (3 if y > 0 else 0)) * COLS, COLS), :]

    for y in range(-1, ROWS + 1):
        here = pl.ds((y + 1) * COLS, COLS)
        p[here, :] = rows(1, s, y) + on_r * r[here, :] + on_v * v[here, :]
        q[here, :] = on_s * rows(2, c, y) + on_u * u[here, :]
    for right in (False, True):
        z = COLS - 1 if right else 0
        change, change_v, change_in, change_u = [side[pl.ds((10 * right + i) * TALL, TALL), :] for i in range(6, 10)]
        zin = z - 1 if right else 1
        for ref, col, value in (
            (p, z, on_r * change + on_v * change_v),
            (p, zin, on_v * change_in),
            (q, z, on_u * change_u),
        ):
            here = pl.ds(COLS + col, ROWS, stride=COLS)
            ref[here, :] = ref[here, :] + value[:ROWS]
            last = pl.ds((ROWS + 1) * COLS + col, 1)
            ref[last, :] = ref[last, :] + value[ROWS : ROWS + 1]
            ref[pl.ds(col, 1), :] = ref[pl.ds(col, 1), :] + value[TALL - 1 :]
    own = pl.ds(COLS, ROWS * COLS)
    sent = [
        pltpu.make_async_copy(p.at[own], prob_out, sems.at[0]),
        pltpu.make_async_copy(q.at[own], adj_out, sems.at[1]),
    ]
    for copy in sent:
        copy.start()
    outer = []
    for right in (False, True):
        z = COLS - 1 if right else 0
        ko, so, co, ro, vo, uo = [side[pl.ds((10 * right + i) * TALL, ROWS), :] for i in range(6)]
        share = ko * recip_sum(column(k, z), ko)
        po, qo = so + on_r * ro + on_v * vo, on_s * co + on_u * uo
        outer.append(-2.0 * (column(p, z, 1) - po) * (column(q, z, 1) - qo) * share * share)

    def share_of(i, y):
        return shares[pl.ds((i * ROWS + y) * COLS, COLS), :]

    insides = [below((COLS, LANES), axis, n - 1) for axis, n in ((0, COLS), (1, LANES))]
    up = None
    for y in range(-1, ROWS):
        pp, qq = row(p, y + 1), row(q, y + 1)
        product = (pp - row(p, y + 2)) * (qq - row(q, y + 2))
        if 0 <= y < ROWS - 1:
            far = share_of(2, y)
            near = 1.0 - far
        else:
            kk, kn = rows(0, k, y), rows(0, k, y + 1)
            share = recip_sum(kk, kn)
            far, near = kn * share, kk * share
        down, up = up, near * near * product
        if y < 0:
            continue
        out = down + far * far * product
        for i, axis in ((0, 1), (1, 0)):
            product = (pp - after(pp, axis)) * (qq - after(qq, axis))
            far = share_of(i, y)
            near = insides[axis] - far
            out = out + far * far * product + before(near * near * product, axis)
        out = -2.0 * out
        grad[pl.ds(y * COLS, COLS), :] = out
        if y % CHUNK == CHUNK - 1:
            at = y + 1 - CHUNK
            for z, value in zip((0, COLS - 1), outer):
                here = pl.ds(at * COLS + z, CHUNK, stride=COLS)
                grad[here, :] = grad[here, :] + value[at : at + CHUNK]
            here = pl.ds(at * COLS, CHUNK * COLS)
            sent.append(pltpu.make_async_copy(grad.at[here], grad_out.at[here], sems.at[2 + at // CHUNK]))
            sent[-1].start()
    for copy in sent:
        copy.wait()


def per_device(*arguments):
    k, sd, lb, s, c = [a.reshape(ROWS * COLS, LANES) for a in arguments]
    vmem = pl.BlockSpec(memory_space=pltpu.VMEM)
    big = pltpu.CompilerParams(vmem_limit_bytes=40 * 1024 * 1024)

    def f32(*rows):
        return tuple(jax.ShapeDtypeStruct((n, LANES), jnp.float32) for n in rows)

    def cost(us):
        return pl.CostEstimate(flops=0, bytes_accessed=int(us * 3.0e6), transcendentals=0)

    far = [pltpu.with_memory_space_constraint(a, pltpu.HBM) for a in (k, s, c, sd, lb)]
    two, one = pl.pallas_call(
        pack_kernel,
        out_shape=f32(ROW_MESSAGE, ROW_MESSAGE),
        in_specs=[pl.BlockSpec(memory_space=pltpu.HBM)] * 5,
        out_specs=(vmem,) * 2,
        scratch_shapes=[
            pltpu.VMEM((3, 6 * COLS, LANES), jnp.float32),
            pltpu.VMEM((2, 6 * COLS, LANES), jnp.int32),
            pltpu.SemaphoreType.DMA((10,)),
        ],
        compiler_params=pltpu.CompilerParams(vmem_limit_bytes=16 * 1024 * 1024),
        name="pack",
    )(*far)
    one, two = swap(one, two, GY)
    block, framed = ROWS * COLS, (ROWS + 2) * COLS
    k, s, c, sd, wx, wy, wz, r, v, u, shares = pl.pallas_call(
        block_kernel,
        out_shape=f32(*(block,) * 3) + (jax.ShapeDtypeStruct((block, LANES), jnp.int32),) + f32(*(block,) * 6, 3 * block),
        in_specs=[pl.BlockSpec(memory_space=pltpu.HBM)] * 5,
        out_specs=(vmem,) * 11,
        scratch_shapes=[pltpu.VMEM((block, LANES), jnp.int32), pltpu.SemaphoreType.DMA((5, ROWS // CHUNK))],
        compiler_params=big,
        cost_estimate=cost(3.0),
        name="block",
    )(*far)
    r, v, u, low, cols, ztwo, zone = pl.pallas_call(
        rows_kernel,
        out_shape=f32(framed, framed, framed, COLS, 10 * TALL + 6 * COLS, COL_MESSAGE, COL_MESSAGE),
        in_specs=[vmem] * 12,
        out_specs=(vmem,) * 7,
        compiler_params=big,
        cost_estimate=cost(0.5),
        name="rows",
    )(two, one, k, s, c, sd, wx, wy, wz, r, v, u)
    zone, ztwo = swap(zone, ztwo, GZ)
    (sums,) = pl.pallas_call(
        inner_kernel,
        out_shape=f32(64),
        in_specs=[vmem] * 9,
        out_specs=(vmem,),
        compiler_params=big,
        cost_estimate=cost(1.0),
        name="inner",
    )(c, sd, wx, wy, wz, low, r, v, u)
    side, line = pl.pallas_call(
        columns_kernel,
        out_shape=f32(20 * TALL, 1),
        in_specs=[vmem] * 10,
        out_specs=(vmem,) * 2,
        compiler_params=big,
        cost_estimate=cost(0.5),
        name="columns",
    )(ztwo, zone, cols, c, sd, wz, sums, r, v, u)
    parts = from_all(jnp.sum(from_all(line, GY + ("gz_1",)), axis=0), ("gz_0",))
    outs = pl.pallas_call(
        finish_kernel,
        out_shape=f32(block, block, block),
        in_specs=[vmem] * 10,
        out_specs=(pl.BlockSpec(memory_space=pltpu.HBM),) * 3,
        scratch_shapes=[
            pltpu.VMEM((framed, LANES), jnp.float32),
            pltpu.VMEM((framed, LANES), jnp.float32),
            pltpu.VMEM((block, LANES), jnp.float32),
            pltpu.SemaphoreType.DMA((2 + ROWS // CHUNK,)),
        ],
        compiler_params=big,
        name="finish",
    )(k, s, c, shares, cols, side, r, v, u, parts)
    return tuple(a.reshape(ROWS, COLS, LANES) for a in outs)


def solution(mesh):
    split = Mesh(mesh.devices.reshape(4, 4, 16, 2), ("gy_0", "gy_1", "gz_0", "gz_1"))
    spec = P(GY, GZ, None)
    return jax.shard_map(per_device, mesh=split, in_specs=(spec,) * 5, out_specs=(spec,) * 3, check_vma=False)
```

```python
import jax
import jax.numpy as jnp
from jax import lax
from jax.experimental import pallas as pl
from jax.experimental.pallas import tpu as pltpu
from jax.sharding import Mesh
from jax.sharding import PartitionSpec as P

GY = ("gy_0", "gy_1")
GZ = ("gz_0", "gz_1")

seed_pull = 4.0
screening = 0.05

ROWS, COLS, LANES = 16, 32, 128
TALL = 24
PARTS = 7
ROW_MESSAGE = PARTS * COLS + 8
COL_MESSAGE = PARTS * ROWS + 16
CHUNK = 4


def swap(even_pairs, odd_pairs, axis):
    n = lax.axis_size(axis)

    def pairs(begin):
        return [p for i in range(begin, n - 1, 2) for p in ((i, i + 1), (i + 1, i))]

    odd_pairs = lax.ppermute(odd_pairs, axis, pairs(1))
    return lax.ppermute(even_pairs, axis, pairs(0)), odd_pairs


def from_all(shard, axis):
    copies = jnp.broadcast_to(shard, (lax.axis_size(axis), *shard.shape))
    return lax.all_to_all(copies, axis, split_axis=0, concat_axis=0, tiled=True)


def recip_sum(first, second):
    return 1.0 / jnp.maximum(first + second, 1e-30)


def harmonic(first, second):
    return 2.0 * first * second * recip_sum(first, second)


def after(a, axis):
    return pltpu.roll(a, a.shape[axis] - 1, axis)


def before(a, axis):
    return pltpu.roll(a, 1, axis)


def below(shape, axis, limit):
    return jnp.where(lax.broadcasted_iota(jnp.int32, shape, axis) < limit, 1.0, 0.0)


def row(ref, y):
    return ref[pl.ds(y * COLS, COLS), :]


def column(ref, z, skip=0):
    return ref[pl.ds(skip * COLS + z, ROWS, stride=COLS), :]


def within(k):
    wx = harmonic(k, after(k, 1)) * below(k.shape, 1, LANES - 1)
    wz = harmonic(k, after(k, 0)) * below(k.shape, 0, COLS - 1)
    return wx, wz


def in_row(f, wx, wz, base):
    fx = wx * (f - after(f, 1))
    fz = wz * (f - after(f, 0))
    return base * f + fx - before(fx, 1) + fz - before(fz, 0)


def base_of(seeds):
    return seed_pull * seeds.astype(jnp.float32) + screening


def pull_of(seeds, labels):
    return seed_pull * (seeds * labels).astype(jnp.float32)


def is_odd(axis):
    return lax.rem(lax.axis_index(axis), 2) == 1


def pack_kernel(k, s, c, sd, lb, two_out, one_out, floats, ints, sems):
    odd_row = lax.rem(lax.axis_index("gy_1"), 2)
    running = []
    for end in range(2):
        at = end * (ROWS - 3) * COLS
        for i, field in enumerate((k, s, c)):
            running.append((field.at[pl.ds(at, 3 * COLS)], floats.at[i, pl.ds(end * 3 * COLS, 3 * COLS)]))
        for i, field in enumerate((sd, lb)):
            running.append((field.at[pl.ds(at, 3 * COLS)], ints.at[i, pl.ds(end * 3 * COLS, 3 * COLS)]))
    running = [pltpu.make_async_copy(src, dst, sems.at[i]) for i, (src, dst) in enumerate(running)]
    for one in running:
        one.start()
    for one in running:
        one.wait()
    for slot, out in enumerate((one_out, two_out)):
        first = odd_row if slot == 0 else 1 - odd_row
        places = [pl.multiple_of((first * i + (1 - first) * (5 - i)) * COLS, COLS) for i in range(3)]
        k0, k1, k2 = [floats[0, pl.ds(p, COLS)] for p in places]
        s0, s1, s2 = [floats[1, pl.ds(p, COLS)] for p in places]
        c0, c1, _ = [floats[2, pl.ds(p, COLS)] for p in places]
        seeds0, seeds1, _ = [ints[0, pl.ds(p, COLS)] for p in places]
        labels0, labels1, _ = [ints[1, pl.ds(p, COLS)] for p in places]
        (wx0, wz0), (wx1, wz1) = within(k0), within(k1)
        w01, w12 = harmonic(k0, k1), harmonic(k1, k2)
        base0, base1 = base_of(seeds0), base_of(seeds1)
        q0 = pull_of(seeds0, labels0) - (in_row(s0, wx0, wz0, base0) + w01 * (s0 - s1))
        q1 = pull_of(seeds1, labels1) - (in_row(s1, wx1, wz1, base1) + w01 * (s1 - s0) + w12 * (s1 - s2))
        image = in_row(q0, wx0, wz0, base0) + w01 * (q0 - q1)
        image_cot = in_row(c0, wx0, wz0, base0) + w01 * (c0 - c1)
        diagonal = base0 + wx0 + before(wx0, 1) + wz0 + before(wz0, 0) + w01
        for i, part in enumerate((k0, s0, c0, q0, image, image_cot, diagonal)):
            out[pl.ds(i * COLS, COLS), :] = part
        at = lax.broadcasted_iota(jnp.int32, (8, LANES), 0)
        corner = jnp.where(at == 0, k1[0:8], k1[COLS - 8 :])
        corner = jnp.where(at == 1, before(s1[0:8], 0), corner)
        out[pl.ds(PARTS * COLS, 8), :] = jnp.where(at == 6, after(s1[COLS - 8 :], 0), corner)


def edge(here, there, inside=None):
    share = recip_sum(here, there)
    if inside is not None:
        share = share * inside
    return 2.0 * here * there * share, share


def block_kernel(*refs):
    far, (k, s, c, sd, wx_out, wy_out, wz_out, r_out, v_out, u_out, shares_out, lb, sems) = refs[:5], refs[5:]
    coming = [
        [
            pltpu.make_async_copy(a.at[pl.ds(at, CHUNK * COLS)], b.at[pl.ds(at, CHUNK * COLS)], sems.at[i, at // (CHUNK * COLS)])
            for at in range(0, ROWS * COLS, CHUNK * COLS)
        ]
        for i, (a, b) in enumerate(zip(far, (k, s, c, sd, lb)))
    ]
    for chunks in coming:
        for chunk in chunks:
            chunk.start()

    def need(y, *fields):
        if y < ROWS and y % CHUNK == 0:
            for i in fields:
                coming[i][y // CHUNK].wait()

    inside_x = below((COLS, LANES), 1, LANES - 1)
    inside_z = below((COLS, LANES), 0, COLS - 1)
    need(0, 0)
    for y in range(ROWS):
        need(y + 1, 0)
        here = row(k, y)
        edges = [
            (wx_out, edge(here, after(here, 1), inside_x)),
            (wz_out, edge(here, after(here, 0), inside_z)),
        ]
        if y < ROWS - 1:
            edges.append((wy_out, edge(here, row(k, y + 1))))
        for i, (out, (w, share)) in enumerate(edges):
            out[pl.ds(y * COLS, COLS), :] = w
            shares_out[pl.ds((i * ROWS + y) * COLS, COLS), :] = share

    def apply(read, y):
        f = read(y)
        out = in_row(f, row(wx_out, y), row(wz_out, y), base_of(row(sd, y)))
        if y < ROWS - 1:
            out = out + row(wy_out, y) * (f - read(y + 1))
        if y > 0:
            out = out + row(wy_out, y - 1) * (f - read(y - 1))
        return out

    need(0, 1, 2, 3, 4)
    for y in range(ROWS):
        need(y + 1, 1, 2, 3, 4)
        r_out[pl.ds(y * COLS, COLS), :] = pull_of(row(sd, y), row(lb, y)) - apply(lambda i: row(s, i), y)
        u_out[pl.ds(y * COLS, COLS), :] = apply(lambda i: row(c, i), y)
    for y in range(ROWS):
        v_out[pl.ds(y * COLS, COLS), :] = apply(lambda i: row(r_out, i), y)


def tall(own, plus1, plus2, minus2, minus1):
    at = lax.broadcasted_iota(jnp.int32, (8, LANES), 0)
    tail = jnp.where(at == 0, plus1, jnp.where(at == 7, minus1, 0.0))
    if plus2 is not None:
        tail = jnp.where(at == 1, plus2, jnp.where(at == 6, minus2, tail))
    return jnp.concatenate([own, tail], axis=0)


def tail_rows(wide):
    at = lax.broadcasted_iota(jnp.int32, (8, LANES), 0)
    return (at < 2) | (at > 5) if wide else (at < 1) | (at > 6)


def tails_packed(k, s, c, q):
    return [jnp.where(tail_rows(True), k, pltpu.roll(s, 4, 0)), jnp.where(tail_rows(False), c, pltpu.roll(q, 4, 0))]


def tails_unpacked(k_s, c_q):
    pairs = ((k_s, True), (pltpu.roll(k_s, 4, 0), True), (c_q, False), (pltpu.roll(c_q, 4, 0), False))
    return [jnp.where(tail_rows(wide), a, 0.0) for a, wide in pairs]


def rows_kernel(two, one, k, s, c, sd, wx, wy, wz, r_in, v_in, u_in, r, v, u, low_out, cols_out, two_out, one_out):
    odd_row, odd_col = is_odd("gy_1"), is_odd("gz_1")
    kept = pl.ds(COLS, ROWS * COLS)
    r[kept, :], v[kept, :], u[kept, :] = r_in[...], v_in[...], u_in[...]

    def arrived(up, at, size):
        first, second = one[pl.ds(at, size), :], two[pl.ds(at, size), :]
        return jnp.where(odd_row, second, first) if up else jnp.where(odd_row, first, second)

    outer, corners, edges, diagonals = [], [], [], []
    for up in (False, True):
        ko, so, co, qo, image, image_cot, diagonal = [arrived(up, i * COLS, COLS) for i in range(PARTS)]
        corners.append(arrived(up, PARTS * COLS, 8))
        y, inner, inner_edge, beyond = (ROWS - 1, ROWS - 2, ROWS - 2, ROWS) if up else (0, 1, 0, -1)
        here, w = lambda a: pl.ds((a + 1) * COLS, COLS), harmonic(ko, row(k, y))
        edges.append(w)
        outer.append((ko, so, co))
        diagonals.append(diagonal + w)
        change = w * (so - row(s, y))
        q = r[here(y), :] + change
        qo = qo - change
        r[here(y), :] = q
        r[here(beyond), :] = qo
        wxo, wzo = within(ko)
        change_o = -change
        spread = wxo * after(change_o, 1) + before(wxo * change_o, 1) + wzo * after(change_o, 0) + before(wzo * change_o, 0)
        v[here(beyond), :] = image + diagonal * change_o - spread + w * (qo - q)
        u[here(beyond), :] = image_cot + w * (co - row(c, y))
        own = in_row(change, row(wx, y), row(wz, y), base_of(row(sd, y))) + row(wy, inner_edge) * change
        v[here(y), :] = v[here(y), :] + own + w * (q - qo)
        v[here(inner), :] = v[here(inner), :] - row(wy, inner_edge) * change
        u[here(y), :] = u[here(y), :] + w * (row(c, y) - co)
    for i, part in enumerate(outer[0] + outer[1]):
        cols_out[pl.ds(10 * TALL + i * COLS, COLS), :] = part
    low_out[...] = edges[0]

    sides = []
    for right in (False, True):
        z = COLS - 1 if right else 0
        zin = z - 1 if right else 1
        pick = lambda a, z=z: a[z : z + 1]
        ck, cs = (7, 6) if right else (0, 1)
        (kl, sl, cl), (kh, sh, ch) = outer
        kc = tall(column(k, z), pick(kh), corners[1][ck : ck + 1], corners[0][ck : ck + 1], pick(kl))
        sc = tall(column(s, z), pick(sh), corners[1][cs : cs + 1], corners[0][cs : cs + 1], pick(sl))
        cc = tall(column(c, z), pick(ch), None, None, pick(cl))
        kin = tall(column(k, zin), pick(kh, zin), None, None, pick(kl, zin))
        rc, vc, uc = (
            tall(column(f, z, 1), f[pl.ds((ROWS + 1) * COLS + z, 1), :], None, None, f[pl.ds(z, 1), :])
            for f in (r, v, u)
        )
        wxc = harmonic(kc, after(kc, 1)) * below(kc.shape, 1, LANES - 1)
        wyc = harmonic(kc, after(kc, 0))
        dc = wxc + before(wxc, 1) + wyc + before(wyc, 0) + harmonic(kc, kin)
        dc = tall(dc[:ROWS] + base_of(column(sd, z)), pick(diagonals[1]), None, None, pick(diagonals[0]))
        for i, part in enumerate((kc, sc, cc, dc, kin)):
            cols_out[pl.ds((5 * right + i) * TALL, TALL), :] = part
        sides.append((kc, sc, cc, rc, vc, uc, dc))
    packed = [[part[:ROWS] for part in side] + tails_packed(*(part[ROWS:] for part in side[:4])) for side in sides]
    at = 0
    for first, last in zip(*packed):
        here = pl.ds(at, first.shape[0])
        one_out[here, :] = jnp.where(odd_col, first, last)
        two_out[here, :] = jnp.where(odd_col, last, first)
        at += first.shape[0]


def inner_kernel(c, sd, wx, wy, wz, low, r, v, u, sums_out):
    at = lax.broadcasted_iota(jnp.int32, (COLS, LANES), 0)
    mask = jnp.where((at >= 2) & (at < COLS - 2), 1.0, 0.0)
    mask_z = jnp.where((at >= 2) & (at < COLS - 3), 1.0, 0.0)
    sums = [jnp.zeros((COLS, LANES), jnp.float32) for _ in range(8)]
    for y in range(ROWS):
        base = base_of(row(sd, y))
        wxy, wzy = row(wx, y) * mask, row(wz, y) * mask_z
        wyy = (row(wy, y - 1) if y else low[...]) * mask
        for i, first, second in ((0, row(r, y + 1), v), (4, row(c, y), u)):
            image, under = row(second, y + 1), row(second, y)
            dx, dz, dy = image - after(image, 1), image - after(image, 0), image - under
            kept, kept_first = image * mask, first * mask
            sums[i] = sums[i] + kept_first * first
            sums[i + 1] = sums[i + 1] + kept_first * image
            sums[i + 2] = sums[i + 2] + kept * image
            sums[i + 3] = sums[i + 3] + wxy * dx * dx + wzy * dz * dz + wyy * dy * dy + base * kept * image
    for i, total in enumerate(sums):
        sums_out[pl.ds(i * 8, 8), :] = total[0:8] + total[8:16] + total[16:24] + total[24:32]


def columns_kernel(two, one, cols, c, sd, wz, sums, r, v, u, side_out, line_out):
    odd_col = is_odd("gz_1")
    totals = [sums[pl.ds(i * 8, 8), :] for i in range(8)]

    def get(ref, z):
        return tall(column(ref, z, 1), ref[pl.ds((ROWS + 1) * COLS + z, 1), :], None, None, ref[pl.ds(z, 1), :])

    def gather(base, wxc, wyc, pairs, z_edges):
        for i, (first, image, z_terms) in enumerate(zip((pairs[0], pairs[2]), (pairs[1], pairs[3]), z_edges)):
            dx, dy = image - after(image, 1), image - before(image, 0)
            energy = wxc * dx * dx + before(wyc, 0) * dy * dy
            own, energy = image[:ROWS], energy[:ROWS] + base * image[:ROWS] * image[:ROWS]
            for w, other in z_terms:
                dz = own - other[:ROWS]
                energy = energy + w[:ROWS] * dz * dz
            for j, term in enumerate((first * first, first * own, own * own, energy)):
                totals[4 * i + j] = totals[4 * i + j] + term[:8] + term[8:16]

    lanes = below((TALL, LANES), 1, LANES - 1)
    for right in (False, True):
        z, zin, zdeep = (COLS - 1, COLS - 2, COLS - 3) if right else (0, 1, 2)

        def arrived(at, size):
            first, second = one[pl.ds(at, size), :], two[pl.ds(at, size), :]
            return jnp.where(odd_col, second, first) if right else jnp.where(odd_col, first, second)

        tails = tails_unpacked(*(arrived(PARTS * ROWS + at, 8) for at in (0, 8))) + [jnp.zeros((8, LANES), jnp.float32)] * 3
        ko, so, co, qo, image, image_cot, diagonal = [
            jnp.concatenate([arrived(i * ROWS, ROWS), tail], axis=0) for i, tail in enumerate(tails)
        ]
        kc, sc, cc, dc, kin = [cols[pl.ds((5 * right + i) * TALL, TALL), :] for i in range(5)]
        w = harmonic(ko, kc)
        win = harmonic(kc, kin)
        change = w * (so - sc)

        def spread(kk, f):
            wxk, wyk = harmonic(kk, after(kk, 1)) * lanes, harmonic(kk, after(kk, 0))
            return (
                wxk * after(f, 1) + before(wxk * f, 1) + wyk * after(f, 0) + before(wyk * f, 0),
                wxk,
                wyk,
            )

        q = get(r, z) + change
        qo = qo - change
        own, wxc, wyc = spread(kc, change)
        change_v = dc * change - own + w * (q - qo)
        change_in = -win * change
        change_u = w * (cc - co)
        vc, vin, uc = get(v, z) + change_v, get(v, zin) + change_in, get(u, z) + change_u
        uin = get(u, zin)
        other, _, _ = spread(ko, -change)
        vo = image - diagonal * change - other + w * (qo - q)
        uo = image_cot + w * (co - cc)
        for i, part in enumerate((ko, so, co, qo, vo, uo, change, change_v, change_in, change_u)):
            side_out[pl.ds((10 * right + i) * TALL, TALL), :] = part
        wdeep = column(wz, zdeep if right else zin)
        vdeep, udeep = column(v, zdeep, 1), column(u, zdeep, 1)
        outside = ([(w, vo)], [(w, uo)]) if right else ([], [])
        gather(
            base_of(column(sd, z)),
            wxc,
            wyc,
            (q[:ROWS], vc, cc[:ROWS], uc),
            (outside[0] + [(win, vin)], outside[1] + [(win, uin)]),
        )
        gather(
            base_of(column(sd, zin)),
            harmonic(kin, after(kin, 1)) * lanes,
            harmonic(kin, after(kin, 0)),
            (column(r, zin, 1), vin, column(c, zin), uin),
            ([(wdeep, vdeep)], [(wdeep, udeep)]),
        )
    line = jnp.zeros((8, LANES), jnp.float32)
    at = lax.broadcasted_iota(jnp.int32, (8, LANES), 1)
    for i, total in enumerate(totals):
        line = line + jnp.where(at == i, jnp.sum(total, axis=1, keepdims=True), 0.0)
    line_out[...] = jnp.sum(line, axis=0, keepdims=True)


def steps(m0, m1, m2, m3):
    a0 = m0 / m1
    new = a0 * a0 * m2 - m0
    grow = 1.0 + new / m0
    curve = grow * grow * m1 - 2.0 * grow * a0 * m2 + a0 * a0 * m3
    a1 = jnp.where((new > 0.0) & (curve > 0.0), new / curve, 0.0)
    return a0 + a1 * grow, -a1 * a0


def finish_kernel(k, s, c, shares, cols, side, r, v, u, line, prob_out, adj_out, grad_out, p, q, grad, sems):
    total = jnp.sum(line[...], axis=0)
    at = lax.broadcasted_iota(jnp.int32, (1, LANES), 1)
    m = [jnp.sum(jnp.where(at == i, total, 0.0), axis=1, keepdims=True) for i in range(8)]
    m = [jnp.broadcast_to(one, (1, LANES)) for one in m]
    on_r, on_v = steps(*m[:4])
    on_s, on_u = steps(*m[4:])

    def rows(field, ref, y):
        if 0 <= y < ROWS:
            return row(ref, y)
        return cols[pl.ds(10 * TALL + (field + (3 if y > 0 else 0)) * COLS, COLS), :]

    for y in range(-1, ROWS + 1):
        here = pl.ds((y + 1) * COLS, COLS)
        p[here, :] = rows(1, s, y) + on_r * r[here, :] + on_v * v[here, :]
        q[here, :] = on_s * rows(2, c, y) + on_u * u[here, :]
    for right in (False, True):
        z = COLS - 1 if right else 0
        change, change_v, change_in, change_u = [side[pl.ds((10 * right + i) * TALL, TALL), :] for i in range(6, 10)]
        zin = z - 1 if right else 1
        for ref, col, value in (
            (p, z, on_r * change + on_v * change_v),
            (p, zin, on_v * change_in),
            (q, z, on_u * change_u),
        ):
            here = pl.ds(COLS + col, ROWS, stride=COLS)
            ref[here, :] = ref[here, :] + value[:ROWS]
            last = pl.ds((ROWS + 1) * COLS + col, 1)
            ref[last, :] = ref[last, :] + value[ROWS : ROWS + 1]
            ref[pl.ds(col, 1), :] = ref[pl.ds(col, 1), :] + value[TALL - 1 :]
    own = pl.ds(COLS, ROWS * COLS)
    sent = [
        pltpu.make_async_copy(p.at[own], prob_out, sems.at[0]),
        pltpu.make_async_copy(q.at[own], adj_out, sems.at[1]),
    ]
    for copy in sent:
        copy.start()
    outer = []
    for right in (False, True):
        z = COLS - 1 if right else 0
        ko, so, co, ro, vo, uo = [side[pl.ds((10 * right + i) * TALL, ROWS), :] for i in range(6)]
        share = ko * recip_sum(column(k, z), ko)
        po, qo = so + on_r * ro + on_v * vo, on_s * co + on_u * uo
        outer.append(-2.0 * (column(p, z, 1) - po) * (column(q, z, 1) - qo) * share * share)

    def share_of(i, y):
        return shares[pl.ds((i * ROWS + y) * COLS, COLS), :]

    def gives(kk, kn, share, product):
        to_here, to_there = kn * share, kk * share
        return to_here * to_here * product, to_there * to_there * product

    up = None
    for y in range(-1, ROWS):
        kk, pp, qq = rows(0, k, y), row(p, y + 1), row(q, y + 1)
        kn = rows(0, k, y + 1)
        share = share_of(2, y) if 0 <= y < ROWS - 1 else recip_sum(kk, kn)
        here, there = gives(kk, kn, share, -2.0 * (pp - row(p, y + 2)) * (qq - row(q, y + 2)))
        down, up = up, there
        if y < 0:
            continue
        out = down + here
        for i, axis in ((0, 1), (1, 0)):
            product = -2.0 * (pp - after(pp, axis)) * (qq - after(qq, axis))
            here, there = gives(kk, after(kk, axis), share_of(i, y), product)
            out = out + here + before(there, axis)
        grad[pl.ds(y * COLS, COLS), :] = out
        if y % CHUNK == CHUNK - 1:
            at = y + 1 - CHUNK
            for z, value in zip((0, COLS - 1), outer):
                here = pl.ds(at * COLS + z, CHUNK, stride=COLS)
                grad[here, :] = grad[here, :] + value[at : at + CHUNK]
            here = pl.ds(at * COLS, CHUNK * COLS)
            sent.append(pltpu.make_async_copy(grad.at[here], grad_out.at[here], sems.at[2 + at // CHUNK]))
            sent[-1].start()
    for copy in sent:
        copy.wait()


def per_device(*arguments):
    k, sd, lb, s, c = [a.reshape(ROWS * COLS, LANES) for a in arguments]
    vmem = pl.BlockSpec(memory_space=pltpu.VMEM)
    big = pltpu.CompilerParams(vmem_limit_bytes=40 * 1024 * 1024)

    def f32(*rows):
        return tuple(jax.ShapeDtypeStruct((n, LANES), jnp.float32) for n in rows)

    def cost(us):
        return pl.CostEstimate(flops=0, bytes_accessed=int(us * 3.0e6), transcendentals=0)

    far = [pltpu.with_memory_space_constraint(a, pltpu.HBM) for a in (k, s, c, sd, lb)]
    two, one = pl.pallas_call(
        pack_kernel,
        out_shape=f32(ROW_MESSAGE, ROW_MESSAGE),
        in_specs=[pl.BlockSpec(memory_space=pltpu.HBM)] * 5,
        out_specs=(vmem,) * 2,
        scratch_shapes=[
            pltpu.VMEM((3, 6 * COLS, LANES), jnp.float32),
            pltpu.VMEM((2, 6 * COLS, LANES), jnp.int32),
            pltpu.SemaphoreType.DMA((10,)),
        ],
        compiler_params=pltpu.CompilerParams(vmem_limit_bytes=16 * 1024 * 1024),
        name="pack",
    )(*far)
    one, two = swap(one, two, GY)
    block, framed = ROWS * COLS, (ROWS + 2) * COLS
    k, s, c, sd, wx, wy, wz, r, v, u, shares = pl.pallas_call(
        block_kernel,
        out_shape=f32(*(block,) * 3) + (jax.ShapeDtypeStruct((block, LANES), jnp.int32),) + f32(*(block,) * 6, 3 * block),
        in_specs=[pl.BlockSpec(memory_space=pltpu.HBM)] * 5,
        out_specs=(vmem,) * 11,
        scratch_shapes=[pltpu.VMEM((block, LANES), jnp.int32), pltpu.SemaphoreType.DMA((5, ROWS // CHUNK))],
        compiler_params=big,
        cost_estimate=cost(3.0),
        name="block",
    )(*far)
    r, v, u, low, cols, ztwo, zone = pl.pallas_call(
        rows_kernel,
        out_shape=f32(framed, framed, framed, COLS, 10 * TALL + 6 * COLS, COL_MESSAGE, COL_MESSAGE),
        in_specs=[vmem] * 12,
        out_specs=(vmem,) * 7,
        compiler_params=big,
        cost_estimate=cost(0.5),
        name="rows",
    )(two, one, k, s, c, sd, wx, wy, wz, r, v, u)
    zone, ztwo = swap(zone, ztwo, GZ)
    (sums,) = pl.pallas_call(
        inner_kernel,
        out_shape=f32(64),
        in_specs=[vmem] * 9,
        out_specs=(vmem,),
        compiler_params=big,
        cost_estimate=cost(1.0),
        name="inner",
    )(c, sd, wx, wy, wz, low, r, v, u)
    side, line = pl.pallas_call(
        columns_kernel,
        out_shape=f32(20 * TALL, 1),
        in_specs=[vmem] * 10,
        out_specs=(vmem,) * 2,
        compiler_params=big,
        cost_estimate=cost(0.5),
        name="columns",
    )(ztwo, zone, cols, c, sd, wz, sums, r, v, u)
    parts = from_all(jnp.sum(from_all(line, GY + ("gz_1",)), axis=0), ("gz_0",))
    outs = pl.pallas_call(
        finish_kernel,
        out_shape=f32(block, block, block),
        in_specs=[vmem] * 10,
        out_specs=(pl.BlockSpec(memory_space=pltpu.HBM),) * 3,
        scratch_shapes=[
            pltpu.VMEM((framed, LANES), jnp.float32),
            pltpu.VMEM((framed, LANES), jnp.float32),
            pltpu.VMEM((block, LANES), jnp.float32),
            pltpu.SemaphoreType.DMA((2 + ROWS // CHUNK,)),
        ],
        compiler_params=big,
        name="finish",
    )(k, s, c, shares, cols, side, r, v, u, parts)
    return tuple(a.reshape(ROWS, COLS, LANES) for a in outs)


def solution(mesh):
    split = Mesh(mesh.devices.reshape(4, 4, 16, 2), ("gy_0", "gy_1", "gz_0", "gz_1"))
    spec = P(GY, GZ, None)
    return jax.shard_map(per_device, mesh=split, in_specs=(spec,) * 5, out_specs=(spec,) * 3, check_vma=False)
```

```python
import jax
import jax.numpy as jnp
from jax import lax
from jax.experimental import pallas as pl
from jax.experimental.pallas import tpu as pltpu
from jax.sharding import Mesh
from jax.sharding import PartitionSpec as P

GY = ("gy_0", "gy_1")
GZ = ("gz_0", "gz_1")

seed_pull = 4.0
screening = 0.05

ROWS, COLS, LANES = 16, 32, 128
TALL = 24
PARTS = 7
ROW_MESSAGE = PARTS * COLS + 8
COL_MESSAGE = PARTS * ROWS + 16
CHUNK = 4


def swap(even_pairs, odd_pairs, axis):
    n = lax.axis_size(axis)

    def pairs(begin):
        return [p for i in range(begin, n - 1, 2) for p in ((i, i + 1), (i + 1, i))]

    odd_pairs = lax.ppermute(odd_pairs, axis, pairs(1))
    return lax.ppermute(even_pairs, axis, pairs(0)), odd_pairs


def from_all(shard, axis):
    copies = jnp.broadcast_to(shard, (lax.axis_size(axis), *shard.shape))
    return lax.all_to_all(copies, axis, split_axis=0, concat_axis=0, tiled=True)


def recip_sum(first, second):
    return 1.0 / jnp.maximum(first + second, 1e-30)


def harmonic(first, second):
    return 2.0 * first * second * recip_sum(first, second)


def after(a, axis):
    return pltpu.roll(a, a.shape[axis] - 1, axis)


def before(a, axis):
    return pltpu.roll(a, 1, axis)


def below(shape, axis, limit):
    return jnp.where(lax.broadcasted_iota(jnp.int32, shape, axis) < limit, 1.0, 0.0)


def row(ref, y):
    return ref[pl.ds(y * COLS, COLS), :]


def column(ref, z, skip=0):
    return ref[pl.ds(skip * COLS + z, ROWS, stride=COLS), :]


def within(k):
    wx = harmonic(k, after(k, 1)) * below(k.shape, 1, LANES - 1)
    wz = harmonic(k, after(k, 0)) * below(k.shape, 0, COLS - 1)
    return wx, wz


def in_row(f, wx, wz, base):
    fx = wx * (f - after(f, 1))
    fz = wz * (f - after(f, 0))
    return base * f + fx - before(fx, 1) + fz - before(fz, 0)


def base_of(seeds):
    return seed_pull * seeds.astype(jnp.float32) + screening


def pull_of(seeds, labels):
    return seed_pull * (seeds * labels).astype(jnp.float32)


def is_odd(axis):
    return lax.rem(lax.axis_index(axis), 2) == 1


def pack_kernel(k, s, c, sd, lb, two_out, one_out, floats, ints, sems):
    odd_row = lax.rem(lax.axis_index("gy_1"), 2)
    running = []
    for end in range(2):
        at = end * (ROWS - 3) * COLS
        for i, field in enumerate((k, s, c)):
            running.append((field.at[pl.ds(at, 3 * COLS)], floats.at[i, pl.ds(end * 3 * COLS, 3 * COLS)]))
        for i, field in enumerate((sd, lb)):
            running.append((field.at[pl.ds(at, 3 * COLS)], ints.at[i, pl.ds(end * 3 * COLS, 3 * COLS)]))
    running = [pltpu.make_async_copy(src, dst, sems.at[i]) for i, (src, dst) in enumerate(running)]
    for one in running:
        one.start()
    for one in running:
        one.wait()
    for slot, out in enumerate((one_out, two_out)):
        first = odd_row if slot == 0 else 1 - odd_row
        places = [pl.multiple_of((first * i + (1 - first) * (5 - i)) * COLS, COLS) for i in range(3)]
        k0, k1, k2 = [floats[0, pl.ds(p, COLS)] for p in places]
        s0, s1, s2 = [floats[1, pl.ds(p, COLS)] for p in places]
        c0, c1, _ = [floats[2, pl.ds(p, COLS)] for p in places]
        seeds0, seeds1, _ = [ints[0, pl.ds(p, COLS)] for p in places]
        labels0, labels1, _ = [ints[1, pl.ds(p, COLS)] for p in places]
        (wx0, wz0), (wx1, wz1) = within(k0), within(k1)
        w01, w12 = harmonic(k0, k1), harmonic(k1, k2)
        base0, base1 = base_of(seeds0), base_of(seeds1)
        q0 = pull_of(seeds0, labels0) - (in_row(s0, wx0, wz0, base0) + w01 * (s0 - s1))
        q1 = pull_of(seeds1, labels1) - (in_row(s1, wx1, wz1, base1) + w01 * (s1 - s0) + w12 * (s1 - s2))
        image = in_row(q0, wx0, wz0, base0) + w01 * (q0 - q1)
        image_cot = in_row(c0, wx0, wz0, base0) + w01 * (c0 - c1)
        diagonal = base0 + wx0 + before(wx0, 1) + wz0 + before(wz0, 0) + w01
        for i, part in enumerate((k0, s0, c0, q0, image, image_cot, diagonal)):
            out[pl.ds(i * COLS, COLS), :] = part
        at = lax.broadcasted_iota(jnp.int32, (8, LANES), 0)
        corner = jnp.where(at == 0, k1[0:8], k1[COLS - 8 :])
        corner = jnp.where(at == 1, before(s1[0:8], 0), corner)
        out[pl.ds(PARTS * COLS, 8), :] = jnp.where(at == 6, after(s1[COLS - 8 :], 0), corner)


def edge(here, there, inside=None):
    share = recip_sum(here, there)
    if inside is not None:
        share = share * inside
    return 2.0 * here * there * share, share


def block_kernel(*refs):
    far, (k, s, c, sd, wx_out, wy_out, wz_out, r_out, v_out, u_out, shares_out, lb, sems) = refs[:5], refs[5:]
    coming = [
        [
            pltpu.make_async_copy(a.at[pl.ds(at, CHUNK * COLS)], b.at[pl.ds(at, CHUNK * COLS)], sems.at[i, at // (CHUNK * COLS)])
            for at in range(0, ROWS * COLS, CHUNK * COLS)
        ]
        for i, (a, b) in enumerate(zip(far, (k, s, c, sd, lb)))
    ]
    for chunks in coming:
        for chunk in chunks:
            chunk.start()

    def need(y, *fields):
        if y < ROWS and y % CHUNK == 0:
            for i in fields:
                coming[i][y // CHUNK].wait()

    inside_x = below((COLS, LANES), 1, LANES - 1)
    inside_z = below((COLS, LANES), 0, COLS - 1)
    need(0, 0)
    for y in range(ROWS):
        need(y + 1, 0)
        here = row(k, y)
        edges = [
            (wx_out, edge(here, after(here, 1), inside_x)),
            (wz_out, edge(here, after(here, 0), inside_z)),
        ]
        if y < ROWS - 1:
            edges.append((wy_out, edge(here, row(k, y + 1))))
        for i, (out, (w, share)) in enumerate(edges):
            out[pl.ds(y * COLS, COLS), :] = w
            shares_out[pl.ds((i * ROWS + y) * COLS, COLS), :] = share

    def apply(read, y):
        f = read(y)
        out = in_row(f, row(wx_out, y), row(wz_out, y), base_of(row(sd, y)))
        if y < ROWS - 1:
            out = out + row(wy_out, y) * (f - read(y + 1))
        if y > 0:
            out = out + row(wy_out, y - 1) * (f - read(y - 1))
        return out

    need(0, 1, 2, 3, 4)
    for y in range(ROWS):
        need(y + 1, 1, 2, 3, 4)
        r_out[pl.ds(y * COLS, COLS), :] = pull_of(row(sd, y), row(lb, y)) - apply(lambda i: row(s, i), y)
        u_out[pl.ds(y * COLS, COLS), :] = apply(lambda i: row(c, i), y)
    for y in range(ROWS):
        v_out[pl.ds(y * COLS, COLS), :] = apply(lambda i: row(r_out, i), y)


def tall(own, plus1, plus2, minus2, minus1):
    at = lax.broadcasted_iota(jnp.int32, (8, LANES), 0)
    tail = jnp.where(at == 0, plus1, jnp.where(at == 7, minus1, 0.0))
    if plus2 is not None:
        tail = jnp.where(at == 1, plus2, jnp.where(at == 6, minus2, tail))
    return jnp.concatenate([own, tail], axis=0)


def tail_rows(wide):
    at = lax.broadcasted_iota(jnp.int32, (8, LANES), 0)
    return (at < 2) | (at > 5) if wide else (at < 1) | (at > 6)


def tails_packed(k, s, c, q):
    return [jnp.where(tail_rows(True), k, pltpu.roll(s, 4, 0)), jnp.where(tail_rows(False), c, pltpu.roll(q, 4, 0))]


def tails_unpacked(k_s, c_q):
    pairs = ((k_s, True), (pltpu.roll(k_s, 4, 0), True), (c_q, False), (pltpu.roll(c_q, 4, 0), False))
    return [jnp.where(tail_rows(wide), a, 0.0) for a, wide in pairs]


def rows_kernel(two, one, k, s, c, sd, wx, wy, wz, r_in, v_in, u_in, r, v, u, low_out, cols_out, two_out, one_out):
    odd_row, odd_col = is_odd("gy_1"), is_odd("gz_1")
    kept = pl.ds(COLS, ROWS * COLS)
    r[kept, :], v[kept, :], u[kept, :] = r_in[...], v_in[...], u_in[...]

    def arrived(up, at, size):
        first, second = one[pl.ds(at, size), :], two[pl.ds(at, size), :]
        return jnp.where(odd_row, second, first) if up else jnp.where(odd_row, first, second)

    outer, corners, edges, diagonals = [], [], [], []
    for up in (False, True):
        ko, so, co, qo, image, image_cot, diagonal = [arrived(up, i * COLS, COLS) for i in range(PARTS)]
        corners.append(arrived(up, PARTS * COLS, 8))
        y, inner, inner_edge, beyond = (ROWS - 1, ROWS - 2, ROWS - 2, ROWS) if up else (0, 1, 0, -1)
        here, w = lambda a: pl.ds((a + 1) * COLS, COLS), harmonic(ko, row(k, y))
        edges.append(w)
        outer.append((ko, so, co))
        diagonals.append(diagonal + w)
        change = w * (so - row(s, y))
        q = r[here(y), :] + change
        qo = qo - change
        r[here(y), :] = q
        r[here(beyond), :] = qo
        wxo, wzo = within(ko)
        change_o = -change
        spread = wxo * after(change_o, 1) + before(wxo * change_o, 1) + wzo * after(change_o, 0) + before(wzo * change_o, 0)
        v[here(beyond), :] = image + diagonal * change_o - spread + w * (qo - q)
        u[here(beyond), :] = image_cot + w * (co - row(c, y))
        own = in_row(change, row(wx, y), row(wz, y), base_of(row(sd, y))) + row(wy, inner_edge) * change
        v[here(y), :] = v[here(y), :] + own + w * (q - qo)
        v[here(inner), :] = v[here(inner), :] - row(wy, inner_edge) * change
        u[here(y), :] = u[here(y), :] + w * (row(c, y) - co)
    for i, part in enumerate(outer[0] + outer[1]):
        cols_out[pl.ds(10 * TALL + i * COLS, COLS), :] = part
    low_out[...] = edges[0]

    sides = []
    for right in (False, True):
        z = COLS - 1 if right else 0
        zin = z - 1 if right else 1
        pick = lambda a, z=z: a[z : z + 1]
        ck, cs = (7, 6) if right else (0, 1)
        (kl, sl, cl), (kh, sh, ch) = outer
        kc = tall(column(k, z), pick(kh), corners[1][ck : ck + 1], corners[0][ck : ck + 1], pick(kl))
        sc = tall(column(s, z), pick(sh), corners[1][cs : cs + 1], corners[0][cs : cs + 1], pick(sl))
        cc = tall(column(c, z), pick(ch), None, None, pick(cl))
        kin = tall(column(k, zin), pick(kh, zin), None, None, pick(kl, zin))
        rc, vc, uc = (
            tall(column(f, z, 1), f[pl.ds((ROWS + 1) * COLS + z, 1), :], None, None, f[pl.ds(z, 1), :])
            for f in (r, v, u)
        )
        wxc = harmonic(kc, after(kc, 1)) * below(kc.shape, 1, LANES - 1)
        wyc = harmonic(kc, after(kc, 0))
        dc = wxc + before(wxc, 1) + wyc + before(wyc, 0) + harmonic(kc, kin)
        dc = tall(dc[:ROWS] + base_of(column(sd, z)), pick(diagonals[1]), None, None, pick(diagonals[0]))
        for i, part in enumerate((kc, sc, cc, dc, kin)):
            cols_out[pl.ds((5 * right + i) * TALL, TALL), :] = part
        sides.append((kc, sc, cc, rc, vc, uc, dc))
    packed = [[part[:ROWS] for part in side] + tails_packed(*(part[ROWS:] for part in side[:4])) for side in sides]
    at = 0
    for first, last in zip(*packed):
        here = pl.ds(at, first.shape[0])
        one_out[here, :] = jnp.where(odd_col, first, last)
        two_out[here, :] = jnp.where(odd_col, last, first)
        at += first.shape[0]


def inner_kernel(c, sd, wx, wy, wz, low, r, v, u, sums_out):
    at = lax.broadcasted_iota(jnp.int32, (COLS, LANES), 0)
    mask = jnp.where((at >= 2) & (at < COLS - 2), 1.0, 0.0)
    mask_z = jnp.where((at >= 2) & (at < COLS - 3), 1.0, 0.0)
    sums = [jnp.zeros((COLS, LANES), jnp.float32) for _ in range(8)]
    for y in range(ROWS):
        base = base_of(row(sd, y))
        wxy, wzy = row(wx, y) * mask, row(wz, y) * mask_z
        wyy = (row(wy, y - 1) if y else low[...]) * mask
        for i, first, second in ((0, row(r, y + 1), v), (4, row(c, y), u)):
            image, under = row(second, y + 1), row(second, y)
            dx, dz, dy = image - after(image, 1), image - after(image, 0), image - under
            kept, kept_first = image * mask, first * mask
            sums[i] = sums[i] + kept_first * first
            sums[i + 1] = sums[i + 1] + kept_first * image
            sums[i + 2] = sums[i + 2] + kept * image
            sums[i + 3] = sums[i + 3] + wxy * dx * dx + wzy * dz * dz + wyy * dy * dy + base * kept * image
    for i, total in enumerate(sums):
        sums_out[pl.ds(i * 8, 8), :] = total[0:8] + total[8:16] + total[16:24] + total[24:32]


def columns_kernel(two, one, cols, c, sd, wz, sums, r, v, u, side_out, line_out):
    odd_col = is_odd("gz_1")
    totals = [sums[pl.ds(i * 8, 8), :] for i in range(8)]

    def get(ref, z):
        return tall(column(ref, z, 1), ref[pl.ds((ROWS + 1) * COLS + z, 1), :], None, None, ref[pl.ds(z, 1), :])

    def gather(base, wxc, wyc, pairs, z_edges):
        for i, (first, image, z_terms) in enumerate(zip((pairs[0], pairs[2]), (pairs[1], pairs[3]), z_edges)):
            dx, dy = image - after(image, 1), image - before(image, 0)
            energy = wxc * dx * dx + before(wyc, 0) * dy * dy
            own, energy = image[:ROWS], energy[:ROWS] + base * image[:ROWS] * image[:ROWS]
            for w, other in z_terms:
                dz = own - other[:ROWS]
                energy = energy + w[:ROWS] * dz * dz
            for j, term in enumerate((first * first, first * own, own * own, energy)):
                totals[4 * i + j] = totals[4 * i + j] + term[:8] + term[8:16]

    lanes = below((TALL, LANES), 1, LANES - 1)
    for right in (False, True):
        z, zin, zdeep = (COLS - 1, COLS - 2, COLS - 3) if right else (0, 1, 2)

        def arrived(at, size):
            first, second = one[pl.ds(at, size), :], two[pl.ds(at, size), :]
            return jnp.where(odd_col, second, first) if right else jnp.where(odd_col, first, second)

        tails = tails_unpacked(*(arrived(PARTS * ROWS + at, 8) for at in (0, 8))) + [jnp.zeros((8, LANES), jnp.float32)] * 3
        ko, so, co, qo, image, image_cot, diagonal = [
            jnp.concatenate([arrived(i * ROWS, ROWS), tail], axis=0) for i, tail in enumerate(tails)
        ]
        kc, sc, cc, dc, kin = [cols[pl.ds((5 * right + i) * TALL, TALL), :] for i in range(5)]
        w = harmonic(ko, kc)
        win = harmonic(kc, kin)
        change = w * (so - sc)

        def spread(kk, f):
            wxk, wyk = harmonic(kk, after(kk, 1)) * lanes, harmonic(kk, after(kk, 0))
            return (
                wxk * after(f, 1) + before(wxk * f, 1) + wyk * after(f, 0) + before(wyk * f, 0),
                wxk,
                wyk,
            )

        q = get(r, z) + change
        qo = qo - change
        own, wxc, wyc = spread(kc, change)
        change_v = dc * change - own + w * (q - qo)
        change_in = -win * change
        change_u = w * (cc - co)
        vc, vin, uc = get(v, z) + change_v, get(v, zin) + change_in, get(u, z) + change_u
        uin = get(u, zin)
        other, _, _ = spread(ko, -change)
        vo = image - diagonal * change - other + w * (qo - q)
        uo = image_cot + w * (co - cc)
        for i, part in enumerate((ko, so, co, qo, vo, uo, change, change_v, change_in, change_u)):
            side_out[pl.ds((10 * right + i) * TALL, TALL), :] = part
        wdeep = column(wz, zdeep if right else zin)
        vdeep, udeep = column(v, zdeep, 1), column(u, zdeep, 1)
        outside = ([(w, vo)], [(w, uo)]) if right else ([], [])
        gather(
            base_of(column(sd, z)),
            wxc,
            wyc,
            (q[:ROWS], vc, cc[:ROWS], uc),
            (outside[0] + [(win, vin)], outside[1] + [(win, uin)]),
        )
        gather(
            base_of(column(sd, zin)),
            harmonic(kin, after(kin, 1)) * lanes,
            harmonic(kin, after(kin, 0)),
            (column(r, zin, 1), vin, column(c, zin), uin),
            ([(wdeep, vdeep)], [(wdeep, udeep)]),
        )
    line = jnp.zeros((8, LANES), jnp.float32)
    at = lax.broadcasted_iota(jnp.int32, (8, LANES), 1)
    for i, total in enumerate(totals):
        line = line + jnp.where(at == i, jnp.sum(total, axis=1, keepdims=True), 0.0)
    line_out[...] = jnp.sum(line, axis=0, keepdims=True)


def steps(m0, m1, m2, m3):
    a0 = m0 / m1
    new = a0 * a0 * m2 - m0
    grow = 1.0 + new / m0
    curve = grow * grow * m1 - 2.0 * grow * a0 * m2 + a0 * a0 * m3
    a1 = jnp.where((new > 0.0) & (curve > 0.0), new / curve, 0.0)
    return a0 + a1 * grow, -a1 * a0


def finish_kernel(k, s, c, shares, cols, side, r, v, u, line, prob_out, adj_out, grad_out, p, q, grad, sems):
    total = jnp.sum(line[...], axis=0)
    at = lax.broadcasted_iota(jnp.int32, (1, LANES), 1)
    m = [jnp.sum(jnp.where(at == i, total, 0.0), axis=1, keepdims=True) for i in range(8)]
    m = [jnp.broadcast_to(one, (1, LANES)) for one in m]
    on_r, on_v = steps(*m[:4])
    on_s, on_u = steps(*m[4:])

    def rows(field, ref, y):
        if 0 <= y < ROWS:
            return row(ref, y)
        return cols[pl.ds(10 * TALL + (field + (3 if y > 0 else 0)) * COLS, COLS), :]

    own, sent = pl.ds(COLS, ROWS * COLS), []
    for i, (ref, out) in enumerate(((p, prob_out), (q, adj_out))):
        for y in range(-1, ROWS + 1):
            here = pl.ds((y + 1) * COLS, COLS)
            if i == 0:
                ref[here, :] = rows(1, s, y) + on_r * r[here, :] + on_v * v[here, :]
            else:
                ref[here, :] = on_s * rows(2, c, y) + on_u * u[here, :]
        for right in (False, True):
            z = COLS - 1 if right else 0
            zin = z - 1 if right else 1
            change, change_v, change_in, change_u = [side[pl.ds((10 * right + j) * TALL, TALL), :] for j in range(6, 10)]
            added = ((z, on_r * change + on_v * change_v), (zin, on_v * change_in)) if i == 0 else ((z, on_u * change_u),)
            for col, value in added:
                here = pl.ds(COLS + col, ROWS, stride=COLS)
                ref[here, :] = ref[here, :] + value[:ROWS]
                last = pl.ds((ROWS + 1) * COLS + col, 1)
                ref[last, :] = ref[last, :] + value[ROWS : ROWS + 1]
                ref[pl.ds(col, 1), :] = ref[pl.ds(col, 1), :] + value[TALL - 1 :]
        sent.append(pltpu.make_async_copy(ref.at[own], out, sems.at[i]))
        sent[-1].start()
    outer = []
    for right in (False, True):
        z = COLS - 1 if right else 0
        ko, so, co, ro, vo, uo = [side[pl.ds((10 * right + i) * TALL, ROWS), :] for i in range(6)]
        share = ko * recip_sum(column(k, z), ko)
        po, qo = so + on_r * ro + on_v * vo, on_s * co + on_u * uo
        outer.append(-2.0 * (column(p, z, 1) - po) * (column(q, z, 1) - qo) * share * share)

    def share_of(i, y):
        return shares[pl.ds((i * ROWS + y) * COLS, COLS), :]

    def gives(kk, kn, share, product):
        to_here, to_there = kn * share, kk * share
        return to_here * to_here * product, to_there * to_there * product

    up = None
    for y in range(-1, ROWS):
        kk, pp, qq = rows(0, k, y), row(p, y + 1), row(q, y + 1)
        kn = rows(0, k, y + 1)
        share = share_of(2, y) if 0 <= y < ROWS - 1 else recip_sum(kk, kn)
        here, there = gives(kk, kn, share, -2.0 * (pp - row(p, y + 2)) * (qq - row(q, y + 2)))
        down, up = up, there
        if y < 0:
            continue
        out = down + here
        for i, axis in ((0, 1), (1, 0)):
            product = -2.0 * (pp - after(pp, axis)) * (qq - after(qq, axis))
            here, there = gives(kk, after(kk, axis), share_of(i, y), product)
            out = out + here + before(there, axis)
        grad[pl.ds(y * COLS, COLS), :] = out
        if y % CHUNK == CHUNK - 1:
            at = y + 1 - CHUNK
            for z, value in zip((0, COLS - 1), outer):
                here = pl.ds(at * COLS + z, CHUNK, stride=COLS)
                grad[here, :] = grad[here, :] + value[at : at + CHUNK]
            here = pl.ds(at * COLS, CHUNK * COLS)
            sent.append(pltpu.make_async_copy(grad.at[here], grad_out.at[here], sems.at[2 + at // CHUNK]))
            sent[-1].start()
    for copy in sent:
        copy.wait()


def per_device(*arguments):
    k, sd, lb, s, c = [a.reshape(ROWS * COLS, LANES) for a in arguments]
    vmem = pl.BlockSpec(memory_space=pltpu.VMEM)
    big = pltpu.CompilerParams(vmem_limit_bytes=40 * 1024 * 1024)

    def f32(*rows):
        return tuple(jax.ShapeDtypeStruct((n, LANES), jnp.float32) for n in rows)

    def cost(us):
        return pl.CostEstimate(flops=0, bytes_accessed=int(us * 3.0e6), transcendentals=0)

    far = [pltpu.with_memory_space_constraint(a, pltpu.HBM) for a in (k, s, c, sd, lb)]
    two, one = pl.pallas_call(
        pack_kernel,
        out_shape=f32(ROW_MESSAGE, ROW_MESSAGE),
        in_specs=[pl.BlockSpec(memory_space=pltpu.HBM)] * 5,
        out_specs=(vmem,) * 2,
        scratch_shapes=[
            pltpu.VMEM((3, 6 * COLS, LANES), jnp.float32),
            pltpu.VMEM((2, 6 * COLS, LANES), jnp.int32),
            pltpu.SemaphoreType.DMA((10,)),
        ],
        compiler_params=pltpu.CompilerParams(vmem_limit_bytes=16 * 1024 * 1024),
        name="pack",
    )(*far)
    one, two = swap(one, two, GY)
    block, framed = ROWS * COLS, (ROWS + 2) * COLS
    k, s, c, sd, wx, wy, wz, r, v, u, shares = pl.pallas_call(
        block_kernel,
        out_shape=f32(*(block,) * 3) + (jax.ShapeDtypeStruct((block, LANES), jnp.int32),) + f32(*(block,) * 6, 3 * block),
        in_specs=[pl.BlockSpec(memory_space=pltpu.HBM)] * 5,
        out_specs=(vmem,) * 11,
        scratch_shapes=[pltpu.VMEM((block, LANES), jnp.int32), pltpu.SemaphoreType.DMA((5, ROWS // CHUNK))],
        compiler_params=big,
        cost_estimate=cost(3.0),
        name="block",
    )(*far)
    r, v, u, low, cols, ztwo, zone = pl.pallas_call(
        rows_kernel,
        out_shape=f32(framed, framed, framed, COLS, 10 * TALL + 6 * COLS, COL_MESSAGE, COL_MESSAGE),
        in_specs=[vmem] * 12,
        out_specs=(vmem,) * 7,
        compiler_params=big,
        cost_estimate=cost(0.5),
        name="rows",
    )(two, one, k, s, c, sd, wx, wy, wz, r, v, u)
    zone, ztwo = swap(zone, ztwo, GZ)
    (sums,) = pl.pallas_call(
        inner_kernel,
        out_shape=f32(64),
        in_specs=[vmem] * 9,
        out_specs=(vmem,),
        compiler_params=big,
        cost_estimate=cost(1.0),
        name="inner",
    )(c, sd, wx, wy, wz, low, r, v, u)
    side, line = pl.pallas_call(
        columns_kernel,
        out_shape=f32(20 * TALL, 1),
        in_specs=[vmem] * 10,
        out_specs=(vmem,) * 2,
        compiler_params=big,
        cost_estimate=cost(0.5),
        name="columns",
    )(ztwo, zone, cols, c, sd, wz, sums, r, v, u)
    parts = from_all(jnp.sum(from_all(line, GY + ("gz_1",)), axis=0), ("gz_0",))
    outs = pl.pallas_call(
        finish_kernel,
        out_shape=f32(block, block, block),
        in_specs=[vmem] * 10,
        out_specs=(pl.BlockSpec(memory_space=pltpu.HBM),) * 3,
        scratch_shapes=[
            pltpu.VMEM((framed, LANES), jnp.float32),
            pltpu.VMEM((framed, LANES), jnp.float32),
            pltpu.VMEM((block, LANES), jnp.float32),
            pltpu.SemaphoreType.DMA((2 + ROWS // CHUNK,)),
        ],
        compiler_params=big,
        name="finish",
    )(k, s, c, shares, cols, side, r, v, u, parts)
    return tuple(a.reshape(ROWS, COLS, LANES) for a in outs)


def solution(mesh):
    split = Mesh(mesh.devices.reshape(4, 4, 16, 2), ("gy_0", "gy_1", "gz_0", "gz_1"))
    spec = P(GY, GZ, None)
    return jax.shard_map(per_device, mesh=split, in_specs=(spec,) * 5, out_specs=(spec,) * 3, check_vma=False)
```
